512 devices in a mesh: band: 16 (over y, z_hi, core), fft: 32 (over x, z_lo).
Axes of the slice: x: 4, y: 4, z: 16 (z_hi: 2, z_lo: 8; z = z_hi * 8 + z_lo), core: 2. Of those that a mesh axis runs over, the one named last changes fastest.
Arguments:
- trial_block: float32 [128, 200704], P('band', 'fft'), may hold values from -0.013671875 to 0.013671875
- all_bands: float32 [512, 200704], P('band', 'fft'), may hold values from -6 to 6
- potential: float32 [192, 192, 192], P('fft'), may hold values from -1.5 to 1
- positions: int32 [4096], replicated, may hold values from 0 to 36863, as said below
- sphere_slots: int32 [200704], P('fft'), may hold values from 0 to 24575, as said below
Outputs:
- intersection: float32 [512, 128], P(('band', 'fft'))
- projected: float32 [512, 128], P(('band', 'fft'))
The draws below stay inside these ranges and needn't reach their ends.
Inputs may be any that keep to these rules, and one draw needn't show every extreme that they name: `positions`: the 4096 entries are distinct; every column has wrapped frequencies wrap(g1), wrap(g2) in -32 to 31, and all such columns occur once, in any order. `sphere_slots`: each fft device's 6272 entries are distinct and ascending; for each local column c they are exactly the slots whose wrapped g3 runs from -h to h for some h of the column, at least 1.
All inputs are finite; a program needn't handle non-finite values.
Results may differ from the reference program's by a relative error of at most 0.000073.
Values sent between devices are 32-bit elements; how exact they have to be, the bound alone decides.
No kernel may reach another device: no remote copies, remote signals or barrier semaphores. Data moves between devices by JAX's collectives and lax.ppermute only.
A program may use at most 128 MiB of HBM per device.

```python
import math
import jax
import jax.numpy as jnp
from jax import lax

NG = 192
K = 64
ZLEN = 49
COLS_DEV = 128
NPW_DEV = 6272
NPW = 200704
NBLK = 128
NALL = 512
N_FFT = 32


def draw_positions(key, part):
    key = jax.random.fold_in(key, 7)
    shuffle = jax.random.permutation(key, K * K)
    freq_one = shuffle // K - K // 2
    freq_two = shuffle % K - K // 2
    return (freq_one % NG * NG + freq_two % NG).astype(jnp.int32)


def draw_sphere_slots(key, part):
    key = jax.random.fold_in(key, 11)
    spread_max = (ZLEN - 1) // 4
    first_key, second_key = jax.random.split(key, 2)
    offsets = jax.random.randint(first_key, (N_FFT, COLS_DEV), 0, spread_max + 1)
    shuffle = jax.vmap(lambda one_key: jax.random.permutation(one_key, COLS_DEV))(jax.random.split(second_key, N_FFT))
    partner = jnp.take_along_axis(offsets, shuffle, axis=1)
    half_span = (ZLEN - 1) // 2 + offsets - partner
    height = lax.broadcasted_iota(jnp.int32, (N_FFT, NG, COLS_DEV), 1)
    freq_three = height - NG * (height >= NG // 2).astype(jnp.int32)
    valid = jnp.abs(freq_three) <= half_span[:, None, :]
    slot_ids = lax.broadcasted_iota(jnp.int32, (N_FFT, NG * COLS_DEV), 1)
    ranking = jnp.where(valid.reshape(N_FFT, NG * COLS_DEV), slot_ids, slot_ids + NG * COLS_DEV)
    chosen = jnp.sort(ranking, axis=1)[:, :NPW_DEV]
    return chosen.reshape(N_FFT * NPW_DEV).astype(jnp.int32)


def block_levels(own_key, shape, shards, low, top_value):
    def one(axis_at, blocks):
        draws = jax.random.uniform(jax.random.fold_in(jax.random.fold_in(own_key, 6), axis_at), (blocks,), jnp.float32, low / len(shards), top_value / len(shards))
        return jnp.repeat(jnp.exp(draws), shape[axis_at] // blocks).reshape((-1,) + (1,) * (len(shape) - axis_at - 1))

    factor_of = one(*shards[0])
    for cut in shards[1:]:
        factor_of = factor_of * one(*cut)
    return factor_of


def centred(rng, dims, scale, reach, cuts=(), held_as=jnp.bfloat16):
    level = block_levels(rng, dims, cuts, -0.22, 0.18) if cuts else 1.0
    result = jax.random.normal(rng, dims, jnp.float32) * scale * level
    return jnp.minimum(jnp.maximum(result, -reach), reach).astype(held_as)


def setup_inputs(seed: int = 0) -> dict:
    key_list = jax.random.split(jax.random.key(seed), 6)
    return {
        "trial_block": centred(key_list[0], (NBLK, NPW), NPW ** -0.5, 0.013671875, ((0, 16), (1, 32)), jnp.float32),
        "all_bands": centred(key_list[1], (NALL, NPW), 1.0, 6.0, ((0, 16), (1, 32)), jnp.float32),
        "potential": jnp.clip(-1.5 + 2.5 * jax.random.uniform(key_list[2], (NG, NG, NG), jnp.float32) ** block_levels(key_list[2], (NG, NG, NG), ((0, 32),), -0.2, 0.2), -1.5, 1.0),
        "positions": draw_positions(jax.random.fold_in(key_list[5], 71), 0),
        "sphere_slots": draw_sphere_slots(jax.random.fold_in(key_list[5], 71), 0),
    }


def cas_matrix(length):
    row_ids = lax.broadcasted_iota(jnp.int32, (length, length), 0)
    col_ids = lax.broadcasted_iota(jnp.int32, (length, length), 1)
    angle = (row_ids * col_ids % length).astype(jnp.float32) * (2.0 * math.pi / length)
    return (jnp.cos(angle) + jnp.sin(angle)) * (1.0 / math.sqrt(length))

def wrapped(values, length):
    return values - length * (values >= length // 2).astype(jnp.int32)

def reference(trial_block, all_bands, potential, positions, sphere_slots):
    precise = lax.Precision.HIGHEST
    cas_rows = cas_matrix(NG)
    box_half = K // 2
    box_table = cas_rows[(lax.iota(jnp.int32, K) - box_half) % NG]
    cols_dev = K * K // N_FFT
    npw_dev = cols_dev * ZLEN
    device = lax.iota(jnp.int32, K * K * ZLEN) // npw_dev
    height = sphere_slots // cols_dev
    column = device * cols_dev + sphere_slots % cols_dev
    freq_one = wrapped(positions // NG, NG)
    freq_two = wrapped(positions % NG, NG)
    box_index = (freq_one + box_half) * K + (freq_two + box_half)
    freq_three = wrapped(height, NG)
    radial = freq_one * freq_one + freq_two * freq_two
    kinetic = 2.0 * (radial[column] + freq_three * freq_three).astype(jnp.float32) / (K * K)
    box_slot = box_index[column]

    def apply_one(coef_row):
        grid_cols = jnp.zeros((NG, K * K), jnp.float32).at[height, box_slot].set(coef_row)
        z_mixed = jnp.dot(cas_rows, grid_cols, precision=precise)
        box_grid = z_mixed.reshape(NG, K, K)
        y_mixed = jnp.einsum('zab,bv->zav', box_grid, box_table, precision=precise)
        real_field = jnp.einsum('zav,au->zuv', y_mixed, box_table, precision=precise)
        weighted = real_field * potential
        y_back = jnp.einsum('zuv,bv->zub', weighted, box_table, precision=precise)
        x_back = jnp.einsum('zub,au->zab', y_back, box_table, precision=precise)
        back_cols = jnp.dot(cas_rows, x_back.reshape(NG, K * K), precision=precise)
        return back_cols[height, box_slot] + kinetic * coef_row
    applied = lax.map(apply_one, trial_block)
    intersection = jnp.einsum('ag,bg->ab', all_bands, trial_block, precision=precise)
    projected = jnp.einsum('ag,bg->ab', all_bands, applied, precision=precise)
    return (intersection, projected)
```

```python
import functools
import math

import jax
import jax.numpy as jnp
import numpy as np
from jax import lax
from jax.experimental import pallas as pl
from jax.experimental.pallas import tpu as pltpu
from jax.sharding import PartitionSpec as P

K = 64
LANES = 128
F32 = jnp.float32
BF16 = jnp.bfloat16


def cas_matrix(length):
    ids = np.arange(length)
    angle = (ids[:, None] * ids[None, :] % length) * (2.0 * math.pi / length)
    return ((np.cos(angle) + np.sin(angle)) / math.sqrt(length)).astype(np.float32)


def halves(table):
    high = table.astype(jnp.bfloat16)
    low = (table - high.astype(np.float32)).astype(jnp.bfloat16)
    return high, low


def split(values):
    high = values.astype(BF16)
    low = (values - high.astype(F32)).astype(BF16)
    return high, low


def dot(left, right):
    return jnp.dot(left, right, preferred_element_type=F32)


def wrapped(values, length):
    return jnp.where(values >= length // 2, values - length, values)


def take_lanes(row, lanes):
    return jnp.take_along_axis(row, lanes, axis=1, mode="promise_in_bounds")


def column_box(positions, grid_cells):
    first = lax.shift_right_logical(lax.shift_right_logical(positions, 6) * 43691, 17)
    second = positions - first * grid_cells
    return wrapped(first, grid_cells), wrapped(second, grid_cells)


def tables_kernel(grid_cells, slots_ref, positions_ref, where_ref, start_ref, inverse_ref, box_ref):
    rows = slots_ref.shape[0]
    column = slots_ref[...] & (LANES - 1)
    lane_ids = lax.broadcasted_iota(jnp.int32, (LANES, LANES), 0)
    counts = jnp.zeros((LANES, LANES), F32)
    ones = jnp.ones((8, LANES), BF16)
    total = jnp.zeros((8, LANES), F32)
    nt = (((1,), (1,)), ((), ()))
    for row in range(rows):
        hit = (column[row : row + 1, :] == lane_ids).astype(BF16)
        total = total + lax.dot_general(ones, hit, nt, preferred_element_type=F32)
    reach = (total[0:1, :] - 1.0) * 0.5
    height = lax.broadcasted_iota(jnp.int32, (grid_cells, LANES), 0)
    away = jnp.abs(wrapped(height, grid_cells)).astype(F32)
    valid = away <= reach
    valid_one = valid.astype(BF16)
    before = (
        lax.broadcasted_iota(jnp.int32, (LANES, LANES), 0)
        < lax.broadcasted_iota(jnp.int32, (LANES, LANES), 1)
    ).astype(BF16)
    rank = dot(valid_one, before)
    in_row = dot(valid_one, jnp.ones((LANES, LANES), BF16)).astype(BF16)
    below = (
        lax.broadcasted_iota(jnp.int32, (grid_cells, grid_cells), 0)
        > lax.broadcasted_iota(jnp.int32, (grid_cells, grid_cells), 1)
    ).astype(BF16)
    start = dot(below, in_row)
    start_ref[...] = start.astype(jnp.int32)
    where_ref[...] = jnp.where(valid, start + rank, -1.0).astype(jnp.int32)
    first, second = column_box(positions_ref[...], grid_cells)
    box = (first + K // 2) * K + second + K // 2
    box_ref[...] = box
    sources = positions_ref.shape[0]
    blocks = sources
    block_ids = lax.broadcasted_iota(jnp.int32, (blocks, LANES), 0)
    own_lane = lax.broadcasted_iota(jnp.int32, (blocks, LANES), 1).astype(F32)
    inverse = jnp.zeros((2 * blocks, LANES), F32)
    for source in range(sources):
        place = box[source : source + 1, :]
        in_block = lax.shift_right_logical(place, 7) == block_ids
        left = jnp.concatenate(
            [jnp.where(in_block, float(source), 0.0), jnp.where(in_block, own_lane, 0.0)], axis=0
        ).astype(BF16)
        right = ((place & (LANES - 1)) == lane_ids).astype(BF16)
        inverse = inverse + lax.dot_general(left, right, nt, preferred_element_type=F32)
    inverse_ref[...] = inverse.astype(jnp.int32)


def forward_kernel(bands, grid_cells, starts, trial_ref, where_ref, cas_ref, out_ref, dense):
    last = trial_ref.shape[1] // LANES - 1

    def expand(height, carry):
        row = lax.shift_right_logical(starts[height], 7)
        after = jnp.minimum(row + 1, last)
        here = trial_ref[:, pl.ds(pl.multiple_of(row * LANES, LANES), LANES)]
        there = trial_ref[:, pl.ds(pl.multiple_of(after * LANES, LANES), LANES)]
        place = jnp.broadcast_to(where_ref[pl.ds(height, 1), :], (bands, LANES)) - row * LANES
        lanes = place & (LANES - 1)
        value = jnp.where(place < LANES, take_lanes(here, lanes), take_lanes(there, lanes))
        dense[pl.ds(pl.multiple_of(height * bands, bands), bands), :] = jnp.where(
            place < 0, 0.0, value
        )
        return carry

    lax.fori_loop(0, grid_cells, expand, 0, unroll=8)
    for band in range(0, bands, 2):
        pair = jnp.concatenate(
            [dense[pl.ds(band + side, grid_cells, stride=bands), :] for side in range(2)], axis=1
        )
        high, low = split(pair)
        mixed = dot(cas_ref[...], jnp.concatenate([high, low, high], axis=0))
        for side in range(2):
            out_ref[pl.ds(band + side, grid_cells, stride=bands), :] = mixed[
                :, side * LANES : (side + 1) * LANES
            ]


def plane_kernel(
    bands,
    sources,
    inverse_ref,
    box_ref,
    y_ref,
    x_ref,
    x_back_ref,
    y_back_ref,
    potential_ref,
    columns_ref,
    out_ref,
    boxes,
):
    grid_cells = potential_ref.shape[1]
    blocks = sources

    def fill(block, carry):
        source_of = jnp.broadcast_to(inverse_ref[pl.ds(block, 1), :], (bands, LANES))
        lane_of = jnp.broadcast_to(inverse_ref[pl.ds(block + blocks, 1), :], (bands, LANES))
        value = jnp.zeros((bands, LANES), F32)
        for source in range(sources):
            value = jnp.where(
                source_of == source, take_lanes(columns_ref[source, 0], lane_of), value
            )
        boxes[pl.ds(pl.multiple_of(block * bands, bands), bands), :] = value
        return carry

    lax.fori_loop(0, blocks, fill, 0)
    stacked = jnp.concatenate(
        [boxes[pl.ds(band, blocks, stride=bands), :] for band in range(bands)], axis=0
    )
    high, low = split(stacked)
    wide = dot(jnp.concatenate([high, low, high], axis=1), y_ref[...])
    half_width = wide.shape[1] // 2
    potential = potential_ref[0]
    back = []
    for band in range(bands):
        mine = wide[band * blocks : (band + 1) * blocks, :]
        mine = jnp.concatenate([mine[:, :half_width], mine[:, half_width:]], axis=0)
        high, low = split(mine)
        field = dot(x_ref[...], jnp.concatenate([high, low, high], axis=0))
        high, low = split(field[:, :grid_cells] * potential)
        both = dot(x_back_ref[...], high)
        back.append(both[:K] + both[K:] + dot(x_back_ref[:K, :], low))
    total = None
    for side in range(2):
        part = jnp.concatenate(
            [one[side * blocks : (side + 1) * blocks, :] for one in back], axis=0
        )
        high, low = split(part)
        term = dot(high, y_back_ref[side, 0]) + dot(low, y_back_ref[side, 0])
        term = term + dot(high, y_back_ref[side, 1])
        total = term if total is None else total + term
    for band in range(bands):
        boxes[pl.ds(band, blocks, stride=bands), :] = total[band * blocks : (band + 1) * blocks, :]

    def pick(source, carry):
        place = jnp.broadcast_to(box_ref[pl.ds(source, 1), :], (bands, LANES))
        lane_of = place & (LANES - 1)
        block_of = lax.shift_right_logical(place, 7)
        value = jnp.zeros((bands, LANES), F32)
        for block in range(blocks):
            value = jnp.where(
                block_of == block,
                take_lanes(boxes[block * bands : (block + 1) * bands, :], lane_of),
                value,
            )
        out_ref[source, 0] = value
        return carry

    lax.fori_loop(0, sources, pick, 0)


def backward_kernel(
    bands,
    grid_cells,
    starts,
    trial_ref,
    slots_ref,
    own_ref,
    cas_ref,
    returned_ref,
    out_ref,
    dense,
):
    for band in range(0, bands, 2):
        pair = jnp.concatenate(
            [returned_ref[pl.ds(band + side, grid_cells, stride=bands), :] for side in range(2)],
            axis=1,
        )
        high, low = split(pair)
        mixed = dot(cas_ref[...], jnp.concatenate([high, low, high], axis=0))
        for side in range(2):
            dense[pl.ds(band + side, grid_cells, stride=bands), :] = mixed[
                :, side * LANES : (side + 1) * LANES
            ]
    rows = slots_ref.shape[0]
    first, second = column_box(own_ref[...], grid_cells)
    radial = jnp.broadcast_to((first * first + second * second).astype(F32), (bands, LANES))
    for row in range(rows):
        slots = jnp.broadcast_to(slots_ref[row : row + 1, :], (bands, LANES))
        height = wrapped(lax.shift_right_logical(slots, 7), grid_cells)
        around = take_lanes(radial, slots & (LANES - 1))
        kinetic = 2.0 * (around + (height * height).astype(F32)) / (K * K)
        cut = slice(row * LANES, (row + 1) * LANES)
        out_ref[:, cut] = kinetic * trial_ref[:, cut]

    def compact(height, carry):
        values = dense[pl.ds(pl.multiple_of(height * bands, bands), bands), :]
        row = lax.shift_right_logical(starts[height], 7)
        for step in range(2):
            near = row + step
            if step:
                near = jnp.minimum(near, rows - 1)
            slots = jnp.broadcast_to(slots_ref[pl.ds(near, 1), :], (bands, LANES))
            mask = lax.shift_right_logical(slots, 7) == height
            if step:
                mask = mask & (near > row)
            cut = pl.ds(pl.multiple_of(near * LANES, LANES), LANES)
            out_ref[:, cut] += jnp.where(mask, take_lanes(values, slots & (LANES - 1)), 0.0)
        return carry

    lax.fori_loop(0, grid_cells, compact, 0, unroll=4)


def constant_tables(grid_cells):
    cas = cas_matrix(grid_cells)
    box_table = cas[(np.arange(K) - K // 2) % grid_cells]
    high, low = halves(cas)
    cas_three = np.concatenate([high, high, low], axis=1)
    padded = -(-grid_cells // LANES) * LANES
    sides = np.zeros((2, K, 2, padded), np.float32)
    for side in range(2):
        sides[side, :, side, :grid_cells] = box_table
    high, low = halves(sides.reshape(2 * K, 2 * padded))
    y_three = np.concatenate([high, high, low], axis=0)
    order = np.concatenate([np.arange(0, K, 2), np.arange(1, K, 2)])
    high, low = halves(box_table[order])
    x_three = np.concatenate([high, high, low], axis=0).T
    x_back = np.concatenate([high, low], axis=0)
    back = np.zeros((2, grid_cells, 2, K), np.float32)
    for side in range(2):
        back[side, :, side, :] = box_table.T
    high, low = halves(back.reshape(2, grid_cells, 2 * K))
    y_back = np.stack([high, low], axis=1)
    return tuple(jnp.asarray(one) for one in (cas_three, y_three, x_three, x_back, y_back))


def whole(array):
    return pl.BlockSpec(array.shape, lambda *_: (0,) * array.ndim)


def apply_hamiltonian(trial_block, potential, positions, sphere_slots):
    bands, coefs = trial_block.shape
    planes, grid_cells = potential.shape[:2]
    fft_size = lax.axis_size("fft")
    slots = sphere_slots.reshape(coefs // LANES, LANES)
    position_rows = positions.reshape(fft_size, LANES)
    own = lax.dynamic_slice_in_dim(position_rows, lax.axis_index("fft"), 1)
    cas_three, y_three, x_three, x_back, y_back = constant_tables(grid_cells)
    i32 = functools.partial(jax.ShapeDtypeStruct, dtype=jnp.int32)
    f32 = functools.partial(jax.ShapeDtypeStruct, dtype=F32)
    params = pltpu.CompilerParams(vmem_limit_bytes=48 * 2**20)
    where, start, inverse, box = pl.pallas_call(
        functools.partial(tables_kernel, grid_cells),
        out_shape=(
            i32((grid_cells, LANES)),
            i32((grid_cells, LANES)),
            i32((2 * fft_size, LANES)),
            i32((fft_size, LANES)),
        ),
        compiler_params=params,
        name="tables",
    )(slots, position_rows)
    starts = start[:, 0]
    dense_rows = grid_cells * bands
    smem = pl.BlockSpec(memory_space=pltpu.SMEM)
    vmem = pl.BlockSpec(memory_space=pltpu.VMEM)
    mixed = pl.pallas_call(
        functools.partial(forward_kernel, bands, grid_cells),
        out_shape=f32((dense_rows, LANES)),
        in_specs=[smem, vmem, vmem, vmem],
        out_specs=vmem,
        scratch_shapes=[pltpu.VMEM((dense_rows, LANES), F32)],
        compiler_params=params,
        name="forward",
    )(starts, trial_block, where, cas_three)
    gathered = lax.all_to_all(mixed, "fft", 0, 0, tiled=True)
    gathered = gathered.reshape(fft_size, planes, bands, LANES)
    block = pl.BlockSpec((fft_size, 1, bands, LANES), lambda z: (0, z, 0, 0))
    tables = (inverse, box, y_three, x_three, x_back, y_back)
    weighted = pl.pallas_call(
        functools.partial(plane_kernel, bands, fft_size),
        out_shape=f32(gathered.shape),
        grid=(planes,),
        in_specs=[whole(one) for one in tables]
        + [pl.BlockSpec((1, grid_cells, grid_cells), lambda z: (z, 0, 0)), block],
        out_specs=block,
        scratch_shapes=[pltpu.VMEM((fft_size * bands, LANES), F32)],
        compiler_params=params,
        name="planes",
    )(*tables, potential, gathered)
    returned = lax.all_to_all(weighted.reshape(dense_rows, LANES), "fft", 0, 0, tiled=True)
    return pl.pallas_call(
        functools.partial(backward_kernel, bands, grid_cells),
        out_shape=f32((bands, coefs)),
        in_specs=[smem] + [vmem] * 5,
        out_specs=vmem,
        scratch_shapes=[pltpu.VMEM((dense_rows, LANES), F32)],
        compiler_params=params,
        name="backward",
    )(starts, trial_block, slots, own, cas_three, returned)


def contract(all_bands, block):
    gathered = lax.all_gather(block, "band", axis=0, tiled=True)
    products = jnp.einsum("ag,bg->ab", all_bands, gathered, precision=lax.Precision.HIGH)
    parts = lax.all_to_all(products, "fft", 0, 0, tiled=True)
    rows = all_bands.shape[0] // lax.axis_size("fft")
    return jnp.sum(parts.reshape(-1, rows, parts.shape[1]), axis=0)


def per_device(trial_block, all_bands, potential, positions, sphere_slots):
    intersection = contract(all_bands, trial_block)
    applied = apply_hamiltonian(trial_block, potential, positions, sphere_slots)
    projected = contract(all_bands, applied)
    return (intersection, projected)


def solution(mesh):
    placed = (P("band", "fft"), P("band", "fft"), P("fft", None, None), P(), P("fft"))
    return jax.shard_map(
        per_device,
        mesh=mesh,
        in_specs=placed,
        out_specs=(P(("band", "fft"), None), P(("band", "fft"), None)),
        check_vma=False,
    )
```

```python
import functools
import math

import jax
import jax.numpy as jnp
import numpy as np
from jax import lax
from jax.experimental import pallas as pl
from jax.experimental.pallas import tpu as pltpu
from jax.sharding import Mesh
from jax.sharding import PartitionSpec as P

K = 64
LANES = 128
SIZES = (4, 2, 2, 4, 8)
BAND = ("y", "zh", "c")
FFT = ("x", "zl")
SIDE = ("y", "c")
NEAR = ("y", "c", "x")
F32 = jnp.float32
BF16 = jnp.bfloat16


def cas_matrix(length):
    ids = np.arange(length)
    angle = (ids[:, None] * ids[None, :] % length) * (2.0 * math.pi / length)
    return ((np.cos(angle) + np.sin(angle)) / math.sqrt(length)).astype(np.float32)


def halves(table):
    high = table.astype(jnp.bfloat16)
    low = (table - high.astype(np.float32)).astype(jnp.bfloat16)
    return high, low


def split(values):
    high = values.astype(BF16)
    low = (values - high.astype(F32)).astype(BF16)
    return high, low


def dot(left, right):
    return jnp.dot(left, right, preferred_element_type=F32)


def wrapped(values, length):
    return jnp.where(values >= length // 2, values - length, values)


def take_lanes(row, lanes):
    return jnp.take_along_axis(row, lanes, axis=1, mode="promise_in_bounds")


def column_box(positions, grid_cells):
    first = lax.shift_right_logical(lax.shift_right_logical(positions, 6) * 43691, 17)
    second = positions - first * grid_cells
    return wrapped(first, grid_cells), wrapped(second, grid_cells)


def tables_kernel(grid_cells, slots_ref, positions_ref, where_ref, start_ref, inverse_ref, box_ref):
    rows = slots_ref.shape[0]
    column = slots_ref[...] & (LANES - 1)
    lane_ids = lax.broadcasted_iota(jnp.int32, (LANES, LANES), 0)
    counts = jnp.zeros((LANES, LANES), F32)
    ones = jnp.ones((8, LANES), BF16)
    total = jnp.zeros((8, LANES), F32)
    nt = (((1,), (1,)), ((), ()))
    for row in range(rows):
        hit = (column[row : row + 1, :] == lane_ids).astype(BF16)
        total = total + lax.dot_general(ones, hit, nt, preferred_element_type=F32)
    reach = (total[0:1, :] - 1.0) * 0.5
    height = lax.broadcasted_iota(jnp.int32, (grid_cells, LANES), 0)
    away = jnp.abs(wrapped(height, grid_cells)).astype(F32)
    valid = away <= reach
    valid_one = valid.astype(BF16)
    before = (
        lax.broadcasted_iota(jnp.int32, (LANES, LANES), 0)
        < lax.broadcasted_iota(jnp.int32, (LANES, LANES), 1)
    ).astype(BF16)
    rank = dot(valid_one, before)
    in_row = dot(valid_one, jnp.ones((LANES, LANES), BF16)).astype(BF16)
    below = (
        lax.broadcasted_iota(jnp.int32, (grid_cells, grid_cells), 0)
        > lax.broadcasted_iota(jnp.int32, (grid_cells, grid_cells), 1)
    ).astype(BF16)
    start = dot(below, in_row)
    start_ref[...] = start.astype(jnp.int32)
    where_ref[...] = jnp.where(valid, start + rank, -1.0).astype(jnp.int32)
    first, second = column_box(positions_ref[...], grid_cells)
    box = (first + K // 2) * K + second + K // 2
    box_ref[...] = box
    sources = positions_ref.shape[0]
    blocks = sources
    block_ids = lax.broadcasted_iota(jnp.int32, (blocks, LANES), 0)
    own_lane = lax.broadcasted_iota(jnp.int32, (blocks, LANES), 1).astype(F32)
    inverse = jnp.zeros((2 * blocks, LANES), F32)
    for source in range(sources):
        place = box[source : source + 1, :]
        in_block = lax.shift_right_logical(place, 7) == block_ids
        left = jnp.concatenate(
            [jnp.where(in_block, float(source), 0.0), jnp.where(in_block, own_lane, 0.0)], axis=0
        ).astype(BF16)
        right = ((place & (LANES - 1)) == lane_ids).astype(BF16)
        inverse = inverse + lax.dot_general(left, right, nt, preferred_element_type=F32)
    inverse_ref[...] = inverse.astype(jnp.int32)


def forward_kernel(bands, grid_cells, starts, trial_ref, where_ref, cas_ref, out_ref, dense):
    last = trial_ref.shape[1] // LANES - 1

    def expand(height, carry):
        row = lax.shift_right_logical(starts[height], 7)
        after = jnp.minimum(row + 1, last)
        here = trial_ref[:, pl.ds(pl.multiple_of(row * LANES, LANES), LANES)]
        there = trial_ref[:, pl.ds(pl.multiple_of(after * LANES, LANES), LANES)]
        place = jnp.broadcast_to(where_ref[pl.ds(height, 1), :], (bands, LANES)) - row * LANES
        lanes = place & (LANES - 1)
        value = jnp.where(place < LANES, take_lanes(here, lanes), take_lanes(there, lanes))
        dense[pl.ds(pl.multiple_of(height * bands, bands), bands), :] = jnp.where(
            place < 0, 0.0, value
        )
        return carry

    lax.fori_loop(0, grid_cells, expand, 0, unroll=8)
    for band in range(0, bands, 2):
        pair = jnp.concatenate(
            [dense[pl.ds(band + side, grid_cells, stride=bands), :] for side in range(2)], axis=1
        )
        high, low = split(pair)
        mixed = dot(cas_ref[...], jnp.concatenate([high, low, high], axis=0))
        for side in range(2):
            out_ref[pl.ds(band + side, grid_cells, stride=bands), :] = mixed[
                :, side * LANES : (side + 1) * LANES
            ]


def potential_kernel(filter_ref, filter_t_ref, potential_ref, out_ref):
    for plane in range(potential_ref.shape[0]):
        high, low = split(potential_ref[plane])
        rows = dot(filter_ref[...], jnp.concatenate([high, low, high], axis=0))
        high, low = split(rows)
        out_ref[plane] = (
            dot(high, filter_t_ref[0]) + dot(low, filter_t_ref[0]) + dot(high, filter_t_ref[1])
        )


def plane_kernel(
    inverse_ref,
    box_ref,
    y_ref,
    x_ref,
    x_back_ref,
    y_back_ref,
    potential_ref,
    columns_ref,
    out_ref,
    boxes,
):
    sources, planes, bands = columns_ref.shape[:3]
    blocks = sources

    def fill(block, carry):
        source_of = jnp.broadcast_to(inverse_ref[pl.ds(block, 1), :], (bands, LANES))
        lane_of = jnp.broadcast_to(inverse_ref[pl.ds(block + blocks, 1), :], (bands, LANES))
        values = [jnp.zeros((bands, LANES), F32) for _ in range(planes)]
        for source in range(sources):
            here = source_of == source
            for plane in range(planes):
                values[plane] = jnp.where(
                    here, take_lanes(columns_ref[source, plane], lane_of), values[plane]
                )
        for plane in range(planes):
            boxes[plane, pl.ds(pl.multiple_of(block * bands, bands), bands), :] = values[plane]
        return carry

    lax.fori_loop(0, blocks, fill, 0)

    def transform(plane, carry):
        stacked = jnp.concatenate(
            [boxes[plane, pl.ds(band, blocks, stride=bands), :] for band in range(bands)], axis=0
        )
        high, low = split(stacked)
        wide = dot(jnp.concatenate([high, low, high], axis=1), y_ref[...])
        potential = potential_ref[plane]
        potential = jnp.concatenate([potential, potential], axis=1)
        back = []
        for band in range(0, bands, 2):
            pair = []
            for one in (band, band + 1):
                mine = wide[one * blocks : (one + 1) * blocks, :]
                pair.append(jnp.concatenate([mine[:, :LANES], mine[:, LANES:]], axis=0))
            high, low = split(jnp.concatenate(pair, axis=1))
            field = dot(x_ref[...], jnp.concatenate([high, low, high], axis=0))
            high, low = split(field * potential)
            both = dot(x_back_ref[...], high)
            both = both[:K] + both[K:] + dot(x_back_ref[:K, :], low)
            for side in range(2):
                one = both[:, side * LANES : (side + 1) * LANES]
                back.append(jnp.concatenate([one[:blocks], one[blocks:]], axis=1))
        high, low = split(jnp.concatenate(back, axis=0))
        total = dot(high, y_back_ref[0]) + dot(low, y_back_ref[0]) + dot(high, y_back_ref[1])
        for band in range(bands):
            boxes[plane, pl.ds(band, blocks, stride=bands), :] = total[
                band * blocks : (band + 1) * blocks, :
            ]
        return carry

    lax.fori_loop(0, planes, transform, 0)

    def pick(source, carry):
        place = jnp.broadcast_to(box_ref[pl.ds(source, 1), :], (bands, LANES))
        lane_of = place & (LANES - 1)
        block_of = lax.shift_right_logical(place, 7)
        values = [jnp.zeros((bands, LANES), F32) for _ in range(planes)]
        for block in range(blocks):
            here = block_of == block
            for plane in range(planes):
                values[plane] = jnp.where(
                    here,
                    take_lanes(boxes[plane, block * bands : (block + 1) * bands, :], lane_of),
                    values[plane],
                )
        for plane in range(planes):
            out_ref[source, plane] = values[plane]
        return carry

    lax.fori_loop(0, sources, pick, 0)


def backward_kernel(
    bands,
    grid_cells,
    starts,
    trial_ref,
    slots_ref,
    own_ref,
    cas_ref,
    returned_ref,
    out_ref,
    dense,
    packed,
):
    for band in range(0, bands, 2):
        pair = jnp.concatenate(
            [returned_ref[pl.ds(band + side, grid_cells, stride=bands), :] for side in range(2)],
            axis=1,
        )
        high, low = split(pair)
        mixed = dot(cas_ref[...], jnp.concatenate([high, low, high], axis=0))
        for side in range(2):
            dense[pl.ds(band + side, grid_cells, stride=bands), :] = mixed[
                :, side * LANES : (side + 1) * LANES
            ]
    rows = slots_ref.shape[0]
    packed[...] = jnp.zeros_like(packed)

    def compact(height, carry):
        values = dense[pl.ds(pl.multiple_of(height * bands, bands), bands), :]
        row = lax.shift_right_logical(starts[height], 7)
        for step in range(2):
            near = row + step
            if step:
                near = jnp.minimum(near, rows - 1)
            slots = jnp.broadcast_to(slots_ref[pl.ds(near, 1), :], (bands, LANES))
            mask = lax.shift_right_logical(slots, 7) == height
            packed[near] = jnp.where(mask, take_lanes(values, slots & (LANES - 1)), packed[near])
        return carry

    lax.fori_loop(0, grid_cells, compact, 0, unroll=4)
    first, second = column_box(own_ref[...], grid_cells)
    radial = jnp.broadcast_to((first * first + second * second).astype(F32), (bands, LANES))
    parts, _, width = out_ref.shape
    each = width // LANES
    for row in range(parts * each):
        cut = slice(row % each * LANES, (row % each + 1) * LANES)
        if row >= rows:
            out_ref[row // each, :, cut] = jnp.zeros((bands, LANES), F32)
            continue
        slots = jnp.broadcast_to(slots_ref[row : row + 1, :], (bands, LANES))
        height = wrapped(lax.shift_right_logical(slots, 7), grid_cells)
        around = take_lanes(radial, slots & (LANES - 1))
        kinetic = 2.0 * (around + (height * height).astype(F32)) / (K * K)
        trial = trial_ref[:, row * LANES : (row + 1) * LANES]
        out_ref[row // each, :, cut] = packed[row] + kinetic * trial


def constant_tables(grid_cells):
    fine = 2 * K
    cas_three = np.concatenate([halves(cas_matrix(grid_cells))[i] for i in (0, 0, 1)], axis=1)
    theta = (np.arange(fine) + 0.5) / fine
    full = np.arange(grid_cells) / grid_cells
    box = np.arange(K) - K // 2
    angle = 2.0 * math.pi * box[:, None] * theta[None, :]
    box_table = ((np.cos(angle) + np.sin(angle)) / math.sqrt(fine)).astype(np.float32)
    waves = 2.0 * math.pi * np.arange(1, K)
    apart = theta[:, None] - full[None, :]
    project = 1.0 + 2.0 * np.cos(waves[:, None, None] * apart[None]).sum(axis=0)
    edge = 2.0 * math.pi * K
    project = project + np.sin(edge * theta)[:, None] * np.sin(edge * full)[None, :]
    project = (project / grid_cells).astype(np.float32)
    high, low = halves(project)
    filter_three = np.concatenate([high, high, low], axis=1)
    filter_back = np.stack([high.T, low.T])
    sides = np.zeros((2, K, 2, fine), np.float32)
    for side in range(2):
        sides[side, :, side, :] = box_table
    high, low = halves(sides.reshape(2 * K, 2 * fine))
    y_three = np.concatenate([high, high, low], axis=0)
    y_back = np.stack([high.T, low.T])
    order = np.concatenate([np.arange(0, K, 2), np.arange(1, K, 2)])
    high, low = halves(box_table[order])
    x_three = np.concatenate([high, high, low], axis=0).T
    x_back = np.concatenate([high, low], axis=0)
    tables = (cas_three, filter_three, filter_back, y_three, x_three, x_back, y_back)
    return tuple(jnp.asarray(one) for one in tables)


def apply_hamiltonian(trial_block, potential, positions, sphere_slots, pieces):
    parts = pieces.shape[0]
    bands, coefs = trial_block.shape
    planes, grid_cells = potential.shape[:2]
    fft_size = lax.axis_size(FFT)
    rows = coefs // LANES
    slots = sphere_slots.reshape(rows, LANES)
    position_rows = positions.reshape(fft_size, LANES)
    own = lax.dynamic_slice_in_dim(position_rows, lax.axis_index(FFT), 1)
    cas_three, filter_three, filter_back, *plane_tables = constant_tables(grid_cells)
    i32 = functools.partial(jax.ShapeDtypeStruct, dtype=jnp.int32)
    f32 = functools.partial(jax.ShapeDtypeStruct, dtype=F32)
    params = pltpu.CompilerParams(vmem_limit_bytes=48 * 2**20)
    where, start, inverse, box = pl.pallas_call(
        functools.partial(tables_kernel, grid_cells),
        out_shape=(
            i32((grid_cells, LANES)),
            i32((grid_cells, LANES)),
            i32((2 * fft_size, LANES)),
            i32((fft_size, LANES)),
        ),
        compiler_params=params,
        name="tables",
    )(slots, position_rows)
    starts = start[:, 0]
    dense_rows = grid_cells * bands
    smem = pl.BlockSpec(memory_space=pltpu.SMEM)
    vmem = pl.BlockSpec(memory_space=pltpu.VMEM)
    mixed = pl.pallas_call(
        functools.partial(forward_kernel, bands, grid_cells),
        out_shape=f32((dense_rows, LANES)),
        in_specs=[smem, vmem, vmem, vmem],
        out_specs=vmem,
        scratch_shapes=[pltpu.VMEM((dense_rows, LANES), F32)],
        compiler_params=params,
        name="forward",
    )(starts, trial_block, where, cas_three)
    filtered = pl.pallas_call(
        potential_kernel,
        out_shape=f32((planes, 2 * K, 2 * K)),
        compiler_params=params,
        cost_estimate=pl.CostEstimate(flops=4 * 10**9, bytes_accessed=4 * 10**6, transcendentals=0),
        name="filter",
    )(filter_three, filter_back, potential)
    gathered = lax.all_to_all(mixed, FFT, 0, 0, tiled=True)
    gathered, pieces = lax.optimization_barrier((gathered, pieces))
    pieces = lax.all_to_all(pieces, SIDE, 0, 0, tiled=True)
    gathered = gathered.reshape(fft_size, planes, bands, LANES)
    weighted = pl.pallas_call(
        plane_kernel,
        out_shape=f32(gathered.shape),
        scratch_shapes=[pltpu.VMEM((planes, fft_size * bands, LANES), F32)],
        compiler_params=params,
        cost_estimate=pl.CostEstimate(
            flops=25 * 10**9, bytes_accessed=60 * 10**6, transcendentals=0
        ),
        name="planes",
    )(inverse, box, *plane_tables, filtered, gathered)
    weighted, pieces = lax.optimization_barrier((weighted, pieces))
    returned = lax.all_to_all(weighted.reshape(dense_rows, LANES), FFT, 0, 0, tiled=True)
    width = pieces.shape[2]
    joined = pl.pallas_call(
        functools.partial(backward_kernel, bands, grid_cells),
        out_shape=f32((parts, bands, width)),
        in_specs=[smem] + [vmem] * 5,
        out_specs=vmem,
        scratch_shapes=[
            pltpu.VMEM((dense_rows, LANES), F32),
            pltpu.VMEM((rows, bands, LANES), F32),
        ],
        compiler_params=params,
        name="backward",
    )(starts, trial_block, slots, own, cas_three, returned)
    return joined, pieces


def other_half(block):
    return lax.ppermute(block, "zh", ((0, 1), (1, 0)))


def per_device(trial_block, all_bands, potential, positions, sphere_slots):
    parts = lax.axis_size(SIDE)
    bands = trial_block.shape[0]
    rows, coefs = all_bands.shape
    width = -(-coefs // (LANES * parts)) * LANES
    pieces = jnp.concatenate([all_bands, trial_block], axis=0)
    pieces = jnp.pad(pieces, ((0, 0), (0, parts * width - coefs)))
    pieces = pieces.reshape(rows + bands, parts, width).transpose(1, 0, 2)
    applied, pieces = apply_hamiltonian(trial_block, potential, positions, sphere_slots, pieces)
    trial = pieces[:, rows:].reshape(parts * bands, width)
    pieces = pieces[:, :rows].reshape(parts * rows, width)
    applied = lax.all_to_all(applied, SIDE, 0, 0, tiled=True).reshape(parts * bands, width)
    products = []
    for block in (trial, applied):
        block = jnp.concatenate([block, other_half(block)], axis=0)
        products.append(jnp.einsum("ag,bg->ab", pieces, block, precision=lax.Precision.HIGH))
    products = jnp.concatenate(products, axis=1)
    columns = products.shape[1]
    near = lax.all_to_all(products, NEAR, 0, 0, tiled=True)
    near = jnp.sum(near.reshape(lax.axis_size(NEAR), -1, columns), axis=0)
    far = lax.all_to_all(near, "zl", 0, 0, tiled=True)
    total = jnp.sum(far, axis=0).reshape(2, 2, SIZES[0], SIZES[2], bands)
    total = jnp.where(lax.axis_index("zh") == 0, total, total[:, ::-1])
    total = total.transpose(0, 2, 1, 3, 4).reshape(2, 1, -1)
    return (total[0], total[1])


def solution(mesh):
    axes = Mesh(mesh.devices.reshape(SIZES), ("y", "zh", "c", "x", "zl"))
    placed = (P(BAND, FFT), P(BAND, FFT), P(FFT, None, None), P(), P(FFT))
    return jax.shard_map(
        per_device,
        mesh=axes,
        in_specs=placed,
        out_specs=(P(BAND + FFT, None), P(BAND + FFT, None)),
        check_vma=False,
    )
```

```python
import functools
import math

import jax
import jax.numpy as jnp
import numpy as np
from jax import lax
from jax.experimental import pallas as pl
from jax.experimental.pallas import tpu as pltpu
from jax.sharding import Mesh
from jax.sharding import PartitionSpec as P

K = 64
LANES = 128
SIZES = (4, 2, 2, 4, 2, 4)
AXES = ("y", "zh", "c", "x", "l2", "ll")
BAND = ("y", "zh", "c")
FFT = ("x", "l2", "ll")
SIDE = ("y", "c")
NEAR = ("y", "c", "x")
GROUP = ("c", "x", "ll")
BLOCKS = 2
HALF = 4
GANG = BLOCKS * HALF
REACH_ROW, START_ROW, SLOT_ROW, ROWS = 196, 200, 204, 256
F32 = jnp.float32
BF16 = jnp.bfloat16


def cas_matrix(length):
    ids = np.arange(length)
    angle = (ids[:, None] * ids[None, :] % length) * (2.0 * math.pi / length)
    return ((np.cos(angle) + np.sin(angle)) / math.sqrt(length)).astype(np.float32)


def halves(table):
    high = table.astype(jnp.bfloat16)
    low = (table - high.astype(np.float32)).astype(jnp.bfloat16)
    return high, low


def split(values):
    high = values.astype(BF16)
    low = (values - high.astype(F32)).astype(BF16)
    return high, low


def dot(left, right):
    return jnp.dot(left, right, preferred_element_type=F32)


def wrapped(values, length):
    return jnp.where(values >= length // 2, values - length, values)


def take_lanes(row, lanes):
    return jnp.take_along_axis(row, lanes, axis=1, mode="promise_in_bounds")


def column_box(positions, grid_cells):
    first = lax.shift_right_logical(lax.shift_right_logical(positions, 6) * 43691, 17)
    second = positions - first * grid_cells
    return wrapped(first, grid_cells), wrapped(second, grid_cells)


def upper(size):
    ids = [lax.broadcasted_iota(jnp.int32, (size, size), axis) for axis in range(2)]
    return (ids[0] < ids[1]).astype(BF16)


def nt_dot(left, right):
    return lax.dot_general(left, right, (((1,), (1,)), ((), ())), preferred_element_type=F32)


def pack_kernel(
    grid_cells, half, slots_ref, positions_ref, trial_ref, own_ref, send_ref, inverse_ref, box_ref
):
    rows = slots_ref.shape[0]
    first_half = half[0] == 0
    column = slots_ref[...] & (LANES - 1)
    lane_ids = lax.broadcasted_iota(jnp.int32, (LANES, LANES), 0)
    ones = jnp.ones((8, LANES), BF16)
    total = jnp.zeros((8, LANES), F32)
    for row in range(rows):
        hit = (column[row : row + 1, :] == lane_ids).astype(BF16)
        total = total + nt_dot(ones, hit)
    reach = (total - 1.0) * 0.5
    padded = 2 * LANES
    height = lax.broadcasted_iota(jnp.int32, (padded, LANES), 0)
    away = jnp.abs(wrapped(height, grid_cells)).astype(F32)
    valid = ((away <= reach[0:1, :]) & (height < grid_cells)).astype(BF16)
    start = dot(nt_dot(ones, valid).astype(BF16), upper(padded))
    for row in range(rows):
        values = trial_ref[:, row * LANES : (row + 1) * LANES]
        own_ref[row * HALF : (row + 1) * HALF, :] = jnp.where(
            first_half, values[:HALF], values[HALF:]
        )
        send_ref[row * HALF : (row + 1) * HALF, :] = jnp.where(
            first_half, values[HALF:], values[:HALF]
        )
    own_slots = slots_ref[...].astype(F32)
    for packet_ref in (own_ref, send_ref):
        packet_ref[REACH_ROW : REACH_ROW + HALF, :] = reach[:HALF]
        packet_ref[START_ROW : START_ROW + 1, :] = start[:1, :LANES]
        packet_ref[START_ROW + 1 : START_ROW + 2, :] = start[:1, LANES:]
        packet_ref[START_ROW + 2 : SLOT_ROW, :] = jnp.zeros((2, LANES), F32)
        packet_ref[SLOT_ROW : SLOT_ROW + rows, :] = own_slots
        packet_ref[SLOT_ROW + rows :, :] = jnp.zeros((ROWS - SLOT_ROW - rows, LANES), F32)
    first, second = column_box(positions_ref[...], grid_cells)
    box = (first + K // 2) * K + second + K // 2
    box_ref[...] = box
    sources = positions_ref.shape[0]
    blocks = sources
    block_ids = lax.broadcasted_iota(jnp.int32, (blocks, LANES), 0)
    own_lane = lax.broadcasted_iota(jnp.int32, (blocks, LANES), 1).astype(F32)
    inverse = jnp.zeros((2 * blocks, LANES), F32)
    for source in range(sources):
        place = box[source : source + 1, :]
        in_block = lax.shift_right_logical(place, 7) == block_ids
        left = jnp.concatenate(
            [jnp.where(in_block, float(source), 0.0), jnp.where(in_block, own_lane, 0.0)], axis=0
        ).astype(BF16)
        right = ((place & (LANES - 1)) == lane_ids).astype(BF16)
        inverse = inverse + nt_dot(left, right)
    inverse_ref[...] = inverse.astype(jnp.int32)


def z_transform(cas_ref, source_ref, out_ref, grid_cells):
    for block in range(0, GANG, 2):
        pair = jnp.concatenate(
            [source_ref[pl.ds(block + side, grid_cells, stride=GANG), :] for side in range(2)],
            axis=1,
        )
        high, low = split(pair)
        mixed = dot(cas_ref[...], jnp.concatenate([high, low, high], axis=0))
        for side in range(2):
            out_ref[pl.ds(block + side, grid_cells, stride=GANG), :] = mixed[
                :, side * LANES : (side + 1) * LANES
            ]


def forward_kernel(grid_cells, starts, packet_ref, cas_ref, out_ref, places, dense):
    height = lax.broadcasted_iota(jnp.int32, (grid_cells, LANES), 0)
    away = jnp.abs(wrapped(height, grid_cells)).astype(F32)
    ids = [lax.broadcasted_iota(jnp.int32, (grid_cells, grid_cells), axis) for axis in range(2)]
    below = (ids[0] > ids[1]).astype(BF16)
    before = upper(LANES)
    every = jnp.ones((LANES, LANES), BF16)
    for block in range(BLOCKS):
        row = block * ROWS + REACH_ROW
        valid = away <= packet_ref[row : row + 1, :]
        valid_one = valid.astype(BF16)
        rank = dot(valid_one, before).astype(jnp.int32)
        start = dot(below, dot(valid_one, every).astype(BF16)).astype(jnp.int32)
        place = jnp.where(valid, rank + (start & (LANES - 1)), -1)
        for band in range(HALF):
            places[pl.ds(block * HALF + band, grid_cells, stride=GANG), :] = place

    def expand(height, carry):
        rows = [
            block * ROWS + lax.shift_right_logical(starts[block, height], 7) * HALF
            for block in range(BLOCKS)
        ]
        rows = [pl.multiple_of(row, HALF) for row in rows]
        here = jnp.concatenate([packet_ref[pl.ds(row, HALF), :] for row in rows], axis=0)
        there = jnp.concatenate([packet_ref[pl.ds(row + HALF, HALF), :] for row in rows], axis=0)
        cut = pl.ds(pl.multiple_of(height * GANG, GANG), GANG)
        place = places[cut, :]
        lanes = place & (LANES - 1)
        value = jnp.where(place < LANES, take_lanes(here, lanes), take_lanes(there, lanes))
        dense[cut, :] = jnp.where(place < 0, 0.0, value)
        return carry

    lax.fori_loop(0, grid_cells, expand, 0, unroll=4)
    z_transform(cas_ref, dense, out_ref, grid_cells)


def potential_kernel(filter_ref, filter_t_ref, potential_ref, out_ref):
    for plane in range(potential_ref.shape[0]):
        high, low = split(potential_ref[plane])
        rows = dot(filter_ref[...], jnp.concatenate([high, low, high], axis=0))
        high, low = split(rows)
        out_ref[plane] = (
            dot(high, filter_t_ref[0]) + dot(low, filter_t_ref[0]) + dot(high, filter_t_ref[1])
        )


def plane_kernel(
    inverse_ref,
    box_ref,
    y_ref,
    x_ref,
    x_back_ref,
    y_back_ref,
    potential_ref,
    columns_ref,
    out_ref,
    boxes,
    staged,
):
    sources, planes, bands = staged.shape[:3]
    blocks = sources
    cores, runs = bands // HALF, SIZES[5]
    places = [
        (source, plane, core, (((core * SIZES[3] + x) * runs + run) * planes + plane) * GANG + block * HALF)
        for source, (x, block, run) in enumerate(np.ndindex(SIZES[3], BLOCKS, runs))
        for plane in range(planes)
        for core in range(cores)
    ]
    for source, plane, core, row in places:
        staged[source, plane, core * HALF : (core + 1) * HALF] = columns_ref[row : row + HALF, :]

    def fill(block, carry):
        source_of = jnp.broadcast_to(inverse_ref[pl.ds(block, 1), :], (bands, LANES))
        lane_of = jnp.broadcast_to(inverse_ref[pl.ds(block + blocks, 1), :], (bands, LANES))
        values = [jnp.zeros((bands, LANES), F32) for _ in range(planes)]
        for source in range(sources):
            here = source_of == source
            for plane in range(planes):
                values[plane] = jnp.where(
                    here, take_lanes(staged[source, plane], lane_of), values[plane]
                )
        for plane in range(planes):
            boxes[plane, pl.ds(pl.multiple_of(block * bands, bands), bands), :] = values[plane]
        return carry

    lax.fori_loop(0, blocks, fill, 0)

    def transform(plane, carry):
        stacked = jnp.concatenate(
            [boxes[plane, pl.ds(band, blocks, stride=bands), :] for band in range(bands)], axis=0
        )
        high, low = split(stacked)
        wide = dot(jnp.concatenate([high, low, high], axis=1), y_ref[...])
        potential = potential_ref[plane]
        potential = jnp.concatenate([potential, potential], axis=1)
        back = []
        for band in range(0, bands, 2):
            pair = []
            for one in (band, band + 1):
                mine = wide[one * blocks : (one + 1) * blocks, :]
                pair.append(jnp.concatenate([mine[:, :LANES], mine[:, LANES:]], axis=0))
            high, low = split(jnp.concatenate(pair, axis=1))
            field = dot(x_ref[...], jnp.concatenate([high, low, high], axis=0))
            high, low = split(field * potential)
            both = dot(x_back_ref[...], high)
            both = both[:K] + both[K:] + dot(x_back_ref[:K, :], low)
            for side in range(2):
                one = both[:, side * LANES : (side + 1) * LANES]
                back.append(jnp.concatenate([one[:blocks], one[blocks:]], axis=1))
        high, low = split(jnp.concatenate(back, axis=0))
        total = dot(high, y_back_ref[0]) + dot(low, y_back_ref[0]) + dot(high, y_back_ref[1])
        for band in range(bands):
            boxes[plane, pl.ds(band, blocks, stride=bands), :] = total[
                band * blocks : (band + 1) * blocks, :
            ]
        return carry

    lax.fori_loop(0, planes, transform, 0)

    def pick(source, carry):
        place = jnp.broadcast_to(box_ref[pl.ds(source, 1), :], (bands, LANES))
        lane_of = place & (LANES - 1)
        block_of = lax.shift_right_logical(place, 7)
        values = [jnp.zeros((bands, LANES), F32) for _ in range(planes)]
        for block in range(blocks):
            here = block_of == block
            for plane in range(planes):
                values[plane] = jnp.where(
                    here,
                    take_lanes(boxes[plane, block * bands : (block + 1) * bands, :], lane_of),
                    values[plane],
                )
        for plane in range(planes):
            staged[source, plane] = values[plane]
        return carry

    lax.fori_loop(0, sources, pick, 0)
    for source, plane, core, row in places:
        out_ref[row : row + HALF, :] = staged[source, plane, core * HALF : (core + 1) * HALF]


def backward_kernel(
    grid_cells, rows, starts, packet_ref, own_ref, cas_ref, returned_ref, out_ref, dense, packed, slots
):
    z_transform(cas_ref, returned_ref, dense, grid_cells)
    slots[...] = jnp.full(slots.shape, -1, jnp.int32)
    for block in range(BLOCKS):
        first = block * ROWS + SLOT_ROW
        slots[block, :rows] = packet_ref[first : first + rows, :].astype(jnp.int32)
    packed[...] = jnp.zeros_like(packed)

    def for_bands(rows_of):
        return jnp.concatenate([jnp.broadcast_to(row, (HALF, LANES)) for row in rows_of], axis=0)

    def compact(height, carry):
        values = dense[pl.ds(pl.multiple_of(height * GANG, GANG), GANG), :]
        for step in range(2):
            near = [
                lax.shift_right_logical(starts[block, height], 7) + step for block in range(BLOCKS)
            ]
            cuts = [pl.ds(pl.multiple_of(row * HALF, HALF), HALF) for row in near]
            own = for_bands([slots[block, pl.ds(near[block], 1), :] for block in range(BLOCKS)])
            old = jnp.concatenate([packed[block, cuts[block], :] for block in range(BLOCKS)], axis=0)
            mask = lax.shift_right_logical(own, 7) == height
            new = jnp.where(mask, take_lanes(values, own & (LANES - 1)), old)
            for block in range(BLOCKS):
                packed[block, cuts[block], :] = new[block * HALF : (block + 1) * HALF, :]
        return carry

    lax.fori_loop(0, grid_cells, compact, 0, unroll=4)
    first, second = column_box(own_ref[...], grid_cells)
    radial = (first * first + second * second).astype(F32)
    radial = for_bands([radial[block : block + 1, :] for block in range(BLOCKS)])
    parts = out_ref.shape[0] // (SIZES[1] * GANG * 8)
    each = -(-rows // parts)
    for part in range(parts):
        for place in range(8):
            row = part * each + place
            if place >= each or row >= rows:
                value = jnp.zeros((GANG, LANES), F32)
            else:
                own = for_bands([slots[block, row : row + 1, :] for block in range(BLOCKS)])
                height = wrapped(lax.shift_right_logical(own, 7), grid_cells)
                around = take_lanes(radial, own & (LANES - 1))
                kinetic = 2.0 * (around + (height * height).astype(F32)) / (K * K)
                cut = slice(row * HALF, (row + 1) * HALF)
                trial = jnp.concatenate(
                    [packet_ref[block * ROWS + cut.start : block * ROWS + cut.stop, :] for block in range(BLOCKS)],
                    axis=0,
                )
                value = jnp.concatenate([packed[block, cut, :] for block in range(BLOCKS)], axis=0)
                value = value + kinetic * trial
            for zh in range(SIZES[1]):
                to = (part // SIZES[2] * SIZES[1] + zh) * SIZES[2] + part % SIZES[2]
                out_ref[pl.ds(to * GANG * 8 + place, GANG, stride=8), :] = value


def constant_tables(grid_cells):
    fine = 2 * K
    order = np.arange(grid_cells).reshape(SIZES[3], SIZES[2], SIZES[5], -1)
    order = order.transpose(1, 0, 2, 3).reshape(-1)
    high, low = halves(cas_matrix(grid_cells))
    cas_out = np.concatenate([high[order], high[order], low[order]], axis=1)
    cas_back = np.concatenate([high[:, order], high[:, order], low[:, order]], axis=1)
    theta = (np.arange(fine) + 0.5) / fine
    full = np.arange(grid_cells) / grid_cells
    box = np.arange(K) - K // 2
    angle = 2.0 * math.pi * box[:, None] * theta[None, :]
    box_table = ((np.cos(angle) + np.sin(angle)) / math.sqrt(fine)).astype(np.float32)
    waves = 2.0 * math.pi * np.arange(1, K)
    apart = theta[:, None] - full[None, :]
    project = 1.0 + 2.0 * np.cos(waves[:, None, None] * apart[None]).sum(axis=0)
    edge = 2.0 * math.pi * K
    project = project + np.sin(edge * theta)[:, None] * np.sin(edge * full)[None, :]
    project = (project / grid_cells).astype(np.float32)
    high, low = halves(project)
    filter_three = np.concatenate([high, high, low], axis=1)
    filter_back = np.stack([high.T, low.T])
    sides = np.zeros((2, K, 2, fine), np.float32)
    for side in range(2):
        sides[side, :, side, :] = box_table
    high, low = halves(sides.reshape(2 * K, 2 * fine))
    y_three = np.concatenate([high, high, low], axis=0)
    y_back = np.stack([high.T, low.T])
    order = np.concatenate([np.arange(0, K, 2), np.arange(1, K, 2)])
    high, low = halves(box_table[order])
    x_three = np.concatenate([high, high, low], axis=0).T
    x_back = np.concatenate([high, low], axis=0)
    tables = (cas_out, cas_back, filter_three, filter_back, y_three, x_three, x_back, y_back)
    return tuple(jnp.asarray(one) for one in tables)


def swap_pairs(turn):
    place = np.arange(math.prod(SIZES)).reshape(SIZES)
    pairs = []
    for (y, zh, c, x, l2, ll), target in np.ndenumerate(place):
        near = zh if l2 == c else (zh * 2 + l2 + turn) % 4 // 2
        pairs.append((int(place[y, near, l2, x, c, ll]), int(target)))
    return tuple(pairs)


def swapped(block, axis):
    return lax.ppermute(block, axis, ((0, 1), (1, 0)))


def apply_hamiltonian(trial_block, potential, positions, sphere_slots, pieces):
    bands, coefs = trial_block.shape
    planes, grid_cells = potential.shape[:2]
    fft_size = lax.axis_size(FFT)
    rows = coefs // LANES
    slots = sphere_slots.reshape(rows, LANES)
    position_rows = positions.reshape(fft_size, LANES)
    own = position_rows.reshape(SIZES[3], BLOCKS, SIZES[5], LANES)
    own = lax.dynamic_index_in_dim(own, lax.axis_index("x"), 0, keepdims=False)
    own = lax.dynamic_index_in_dim(own, lax.axis_index("ll"), 1, keepdims=False)
    cas_out, cas_back, filter_three, filter_back, *plane_tables = constant_tables(grid_cells)
    i32 = functools.partial(jax.ShapeDtypeStruct, dtype=jnp.int32)
    f32 = functools.partial(jax.ShapeDtypeStruct, dtype=F32)
    params = pltpu.CompilerParams(vmem_limit_bytes=48 * 2**20)
    smem = pl.BlockSpec(memory_space=pltpu.SMEM)
    vmem = pl.BlockSpec(memory_space=pltpu.VMEM)
    filtered = pl.pallas_call(
        potential_kernel,
        out_shape=f32((planes, 2 * K, 2 * K)),
        compiler_params=params,
        name="filter",
    )(filter_three, filter_back, potential)
    filtered, trial_block = lax.optimization_barrier((filtered, trial_block))
    cut = planes // 2
    filtered = [
        lax.ppermute(part, BAND + FFT, swap_pairs(turn))
        for part, turn in ((filtered[:cut], 1), (filtered[cut:], -1))
    ]
    half = lax.axis_index("l2")
    packet = f32((ROWS, LANES))
    kept, sent, inverse, box = pl.pallas_call(
        functools.partial(pack_kernel, grid_cells),
        out_shape=(packet, packet, i32((2 * fft_size, LANES)), i32((fft_size, LANES))),
        in_specs=[smem] + [vmem] * 3,
        out_specs=[vmem] * 4,
        compiler_params=params,
        name="pack",
    )(half.reshape(1), slots, position_rows, trial_block)
    other = swapped(sent, "l2")
    packet = jnp.where(half == 0, jnp.stack([kept, other]), jnp.stack([other, kept]))
    starts = packet[:, START_ROW : START_ROW + 2].reshape(BLOCKS, -1).astype(jnp.int32)
    packet = packet.reshape(BLOCKS * ROWS, LANES)
    dense_rows = grid_cells * GANG
    dense = pltpu.VMEM((dense_rows, LANES), F32)
    mixed = pl.pallas_call(
        functools.partial(forward_kernel, grid_cells),
        out_shape=f32((dense_rows, LANES)),
        in_specs=[smem, vmem, vmem],
        out_specs=vmem,
        scratch_shapes=[pltpu.VMEM((dense_rows, LANES), jnp.int32), dense],
        compiler_params=params,
        name="forward",
    )(starts, packet, cas_out)
    filtered = jnp.concatenate(filtered, axis=0)
    pieces = lax.all_to_all(pieces, SIDE, 0, 0, tiled=True)
    mixed, filtered, pieces = lax.optimization_barrier((mixed, filtered, pieces))
    gathered = lax.all_to_all(mixed, GROUP, 0, 0, tiled=True)
    trial = pieces[:, -bands:].reshape(-1, pieces.shape[2])
    gathered, trial = lax.optimization_barrier((gathered, trial))
    theirs = swapped(trial, "zh")
    weighted = pl.pallas_call(
        plane_kernel,
        out_shape=f32(gathered.shape),
        scratch_shapes=[
            pltpu.VMEM((planes, fft_size * bands, LANES), F32),
            pltpu.VMEM((fft_size, planes, bands, LANES), F32),
        ],
        compiler_params=params,
        cost_estimate=pl.CostEstimate(
            flops=25 * 10**9, bytes_accessed=60 * 10**6, transcendentals=0
        ),
        name="planes",
    )(inverse, box, *plane_tables, filtered, gathered)
    weighted, theirs = lax.optimization_barrier((weighted, theirs))
    returned = lax.all_to_all(weighted, GROUP, 0, 0, tiled=True)
    parts = pieces.shape[0]
    tall = rows + 7 & -8
    applied = pl.pallas_call(
        functools.partial(backward_kernel, grid_cells, rows),
        out_shape=f32((SIZES[1] * parts * GANG * 8, LANES)),
        in_specs=[smem] + [vmem] * 4,
        out_specs=vmem,
        scratch_shapes=[
            dense,
            pltpu.VMEM((BLOCKS, tall * HALF, LANES), F32),
            pltpu.VMEM((BLOCKS, tall, LANES), jnp.int32),
        ],
        compiler_params=params,
        cost_estimate=pl.CostEstimate(flops=8 * 10**9, bytes_accessed=16 * 10**6, transcendentals=0),
        name="backward",
    )(starts, packet, own, cas_back, returned)
    applied = lax.all_to_all(applied, BAND + ("l2",), 0, 0, tiled=True)
    each = pieces.shape[2] // LANES
    applied = applied.reshape(-1, 8, LANES)[:, :each].reshape(2 * trial.shape[0], -1)
    return applied, pieces[:, :-bands], jnp.concatenate([trial, theirs], axis=0)


def per_device(trial_block, all_bands, potential, positions, sphere_slots):
    parts = lax.axis_size(SIDE)
    rows, coefs = all_bands.shape
    width = -(-coefs // (LANES * parts)) * LANES
    pieces = jnp.concatenate([all_bands, trial_block], axis=0)
    pieces = jnp.pad(pieces, ((0, 0), (0, parts * width - coefs)))
    pieces = pieces.reshape(-1, parts, width).transpose(1, 0, 2)
    applied, pieces, trial = apply_hamiltonian(trial_block, potential, positions, sphere_slots, pieces)
    pieces = pieces.reshape(parts * rows, width)
    products = [
        jnp.einsum("ag,bg->ab", pieces, block, precision=lax.Precision.HIGH)
        for block in (trial, applied)
    ]
    products = jnp.concatenate(products, axis=1)
    columns = products.shape[1]
    near = lax.all_to_all(products, NEAR, 0, 0, tiled=True)
    near = jnp.sum(near.reshape(lax.axis_size(NEAR), -1, columns), axis=0)
    far = lax.all_to_all(near, ("l2", "ll"), 0, 0, tiled=True)
    total = jnp.sum(far, axis=0).reshape(2, -1)
    first = total[0].reshape(SIZES[1], SIZES[0], SIZES[2], -1)
    first = jnp.where(lax.axis_index("zh") == 0, first, first[::-1]).transpose(1, 0, 2, 3)
    return (first.reshape(1, -1), total[1:])


def solution(mesh):
    axes = Mesh(mesh.devices.reshape(SIZES), AXES)
    placed = (P(BAND, FFT), P(BAND, FFT), P(FFT, None, None), P(), P(FFT))
    return jax.shard_map(
        per_device,
        mesh=axes,
        in_specs=placed,
        out_specs=(P(BAND + FFT, None), P(BAND + FFT, None)),
        check_vma=False,
    )
```

```python
import functools
import math

import jax
import jax.numpy as jnp
import numpy as np
from jax import lax
from jax.experimental import pallas as pl
from jax.experimental.pallas import tpu as pltpu
from jax.sharding import Mesh
from jax.sharding import PartitionSpec as P

K = 64
LANES = 128
SIZES = (4, 2, 2, 4, 2, 4)
AXES = ("y", "zh", "c", "x", "l2", "ll")
BAND = ("y", "zh", "c")
FFT = ("x", "l2", "ll")
SIDE = ("y", "c")
NEAR = ("y", "c", "x")
GROUP = ("c", "x", "ll")
BLOCKS = 2
HALF = 4
GANG = BLOCKS * HALF
REACH_ROW, START_ROW, SLOT_ROW, ROWS = 196, 200, 204, 256
F32 = jnp.float32
BF16 = jnp.bfloat16


def cas_matrix(length):
    ids = np.arange(length)
    angle = (ids[:, None] * ids[None, :] % length) * (2.0 * math.pi / length)
    return ((np.cos(angle) + np.sin(angle)) / math.sqrt(length)).astype(np.float32)


def halves(table):
    high = table.astype(jnp.bfloat16)
    low = (table - high.astype(np.float32)).astype(jnp.bfloat16)
    return high, low


def split(values):
    high = values.astype(BF16)
    low = (values - high.astype(F32)).astype(BF16)
    return high, low


def dot(left, right):
    return jnp.dot(left, right, preferred_element_type=F32)


def wrapped(values, length):
    return jnp.where(values >= length // 2, values - length, values)


def take_lanes(row, lanes):
    return jnp.take_along_axis(row, lanes, axis=1, mode="promise_in_bounds")


def column_box(positions, grid_cells):
    first = lax.shift_right_logical(lax.shift_right_logical(positions, 6) * 43691, 17)
    second = positions - first * grid_cells
    return wrapped(first, grid_cells), wrapped(second, grid_cells)


def upper(size):
    ids = [lax.broadcasted_iota(jnp.int32, (size, size), axis) for axis in range(2)]
    return (ids[0] < ids[1]).astype(BF16)


def nt_dot(left, right):
    return lax.dot_general(left, right, (((1,), (1,)), ((), ())), preferred_element_type=F32)


def pack_kernel(
    grid_cells, half, slots_ref, trial_ref, own_ref, send_ref
):
    rows = slots_ref.shape[0]
    first_half = half[0] == 0
    column = slots_ref[...] & (LANES - 1)
    lane_ids = lax.broadcasted_iota(jnp.int32, (LANES, LANES), 0)
    ones = jnp.ones((8, LANES), BF16)
    total = jnp.zeros((8, LANES), F32)
    for row in range(rows):
        hit = (column[row : row + 1, :] == lane_ids).astype(BF16)
        total = total + nt_dot(ones, hit)
    reach = (total - 1.0) * 0.5
    padded = 2 * LANES
    height = lax.broadcasted_iota(jnp.int32, (padded, LANES), 0)
    away = jnp.abs(wrapped(height, grid_cells)).astype(F32)
    valid = ((away <= reach[0:1, :]) & (height < grid_cells)).astype(BF16)
    start = dot(nt_dot(ones, valid).astype(BF16), upper(padded))
    for row in range(rows):
        values = trial_ref[:, row * LANES : (row + 1) * LANES]
        own_ref[row * HALF : (row + 1) * HALF, :] = jnp.where(
            first_half, values[:HALF], values[HALF:]
        )
        send_ref[row * HALF : (row + 1) * HALF, :] = jnp.where(
            first_half, values[HALF:], values[:HALF]
        )
    own_slots = slots_ref[...].astype(F32)
    for packet_ref in (own_ref, send_ref):
        packet_ref[REACH_ROW : REACH_ROW + HALF, :] = reach[:HALF]
        packet_ref[START_ROW : START_ROW + 1, :] = start[:1, :LANES]
        packet_ref[START_ROW + 1 : START_ROW + 2, :] = start[:1, LANES:]
        packet_ref[START_ROW + 2 : SLOT_ROW, :] = jnp.zeros((2, LANES), F32)
        packet_ref[SLOT_ROW : SLOT_ROW + rows, :] = own_slots
        packet_ref[SLOT_ROW + rows :, :] = jnp.zeros((ROWS - SLOT_ROW - rows, LANES), F32)


def boxes_kernel(grid_cells, positions_ref, inverse_ref, box_ref):
    lane_ids = lax.broadcasted_iota(jnp.int32, (LANES, LANES), 0)
    first, second = column_box(positions_ref[...], grid_cells)
    box = (first + K // 2) * K + second + K // 2
    box_ref[...] = box
    sources = positions_ref.shape[0]
    blocks = sources
    block_ids = lax.broadcasted_iota(jnp.int32, (blocks, LANES), 0)
    own_lane = lax.broadcasted_iota(jnp.int32, (blocks, LANES), 1).astype(F32)
    inverse = jnp.zeros((2 * blocks, LANES), F32)
    for source in range(sources):
        place = box[source : source + 1, :]
        in_block = lax.shift_right_logical(place, 7) == block_ids
        left = jnp.concatenate(
            [jnp.where(in_block, float(source), 0.0), jnp.where(in_block, own_lane, 0.0)], axis=0
        ).astype(BF16)
        right = ((place & (LANES - 1)) == lane_ids).astype(BF16)
        inverse = inverse + nt_dot(left, right)
    inverse_ref[...] = inverse.astype(jnp.int32)


def z_transform(cas_ref, source_ref, out_ref, grid_cells):
    for block in range(0, GANG, 2):
        pair = jnp.concatenate(
            [source_ref[pl.ds(block + side, grid_cells, stride=GANG), :] for side in range(2)],
            axis=1,
        )
        high, low = split(pair)
        mixed = dot(cas_ref[...], jnp.concatenate([high, low, high], axis=0))
        for side in range(2):
            out_ref[pl.ds(block + side, grid_cells, stride=GANG), :] = mixed[
                :, side * LANES : (side + 1) * LANES
            ]


def forward_kernel(grid_cells, starts, packet_ref, cas_ref, out_ref, places, dense):
    height = lax.broadcasted_iota(jnp.int32, (grid_cells, LANES), 0)
    away = jnp.abs(wrapped(height, grid_cells)).astype(F32)
    ids = [lax.broadcasted_iota(jnp.int32, (grid_cells, grid_cells), axis) for axis in range(2)]
    below = (ids[0] > ids[1]).astype(BF16)
    before = upper(LANES)
    every = jnp.ones((LANES, LANES), BF16)
    for block in range(BLOCKS):
        row = block * ROWS + REACH_ROW
        valid = away <= packet_ref[row : row + 1, :]
        valid_one = valid.astype(BF16)
        rank = dot(valid_one, before).astype(jnp.int32)
        start = dot(below, dot(valid_one, every).astype(BF16)).astype(jnp.int32)
        place = jnp.where(valid, rank + (start & (LANES - 1)), -1)
        for band in range(HALF):
            places[pl.ds(block * HALF + band, grid_cells, stride=GANG), :] = place

    def expand(height, carry):
        rows = [
            block * ROWS + lax.shift_right_logical(starts[block, height], 7) * HALF
            for block in range(BLOCKS)
        ]
        rows = [pl.multiple_of(row, HALF) for row in rows]
        here = jnp.concatenate([packet_ref[pl.ds(row, HALF), :] for row in rows], axis=0)
        there = jnp.concatenate([packet_ref[pl.ds(row + HALF, HALF), :] for row in rows], axis=0)
        cut = pl.ds(pl.multiple_of(height * GANG, GANG), GANG)
        place = places[cut, :]
        lanes = place & (LANES - 1)
        value = jnp.where(place < LANES, take_lanes(here, lanes), take_lanes(there, lanes))
        dense[cut, :] = jnp.where(place < 0, 0.0, value)
        return carry

    lax.fori_loop(0, grid_cells, expand, 0, unroll=8)
    z_transform(cas_ref, dense, out_ref, grid_cells)


def potential_kernel(filter_ref, filter_t_ref, potential_ref, out_ref):
    for plane in range(potential_ref.shape[0]):
        high, low = split(potential_ref[plane])
        rows = dot(filter_ref[...], jnp.concatenate([high, low, high], axis=0))
        high, low = split(rows)
        out_ref[plane] = (
            dot(high, filter_t_ref[0]) + dot(low, filter_t_ref[0]) + dot(high, filter_t_ref[1])
        )


def plane_kernel(
    inverse_ref,
    box_ref,
    y_ref,
    x_ref,
    x_back_ref,
    y_back_ref,
    potential_ref,
    columns_ref,
    out_ref,
    boxes,
    staged,
    products,
):
    sources, planes, bands = staged.shape[:3]
    blocks = sources
    cores, runs = bands // HALF, SIZES[5]
    places = [
        (source, plane, core, (((core * SIZES[3] + x) * runs + run) * planes + plane) * GANG + block * HALF)
        for source, (x, block, run) in enumerate(np.ndindex(SIZES[3], BLOCKS, runs))
        for plane in range(planes)
        for core in range(cores)
    ]
    for source, plane, core, row in places:
        staged[source, plane, core * HALF : (core + 1) * HALF] = columns_ref[row : row + HALF, :]

    def fill(block, carry):
        source_of = jnp.broadcast_to(inverse_ref[pl.ds(block, 1), :], (bands, LANES))
        lane_of = jnp.broadcast_to(inverse_ref[pl.ds(block + blocks, 1), :], (bands, LANES))
        values = [jnp.zeros((bands, LANES), F32) for _ in range(planes)]
        for source in range(sources):
            here = source_of == source
            for plane in range(planes):
                values[plane] = jnp.where(
                    here, take_lanes(staged[source, plane], lane_of), values[plane]
                )
        for plane in range(planes):
            boxes[plane, pl.ds(pl.multiple_of(block * bands, bands), bands), :] = values[plane]
        return carry

    lax.fori_loop(0, blocks, fill, 0)

    def transform(plane, carry):
        stacked = jnp.concatenate(
            [boxes[plane, pl.ds(band, blocks, stride=bands), :] for band in range(bands)], axis=0
        )
        high, low = split(stacked)
        wide = dot(jnp.concatenate([high, low, high], axis=1), y_ref[...])
        potential = potential_ref[plane]
        potential = jnp.concatenate([potential, potential], axis=1)
        back = []
        for band in range(0, bands, 2):
            pair = []
            for one in (band, band + 1):
                mine = wide[one * blocks : (one + 1) * blocks, :]
                pair.append(jnp.concatenate([mine[:, :LANES], mine[:, LANES:]], axis=0))
            high, low = split(jnp.concatenate(pair, axis=1))
            field = dot(x_ref[...], jnp.concatenate([high, low, high], axis=0))
            high, low = split(field * potential)
            both = dot(x_back_ref[...], high)
            both = both[:K] + both[K:] + dot(x_back_ref[:K, :], low)
            for side in range(2):
                one = both[:, side * LANES : (side + 1) * LANES]
                back.append(jnp.concatenate([one[:blocks], one[blocks:]], axis=1))
        high, low = split(jnp.concatenate(back, axis=0))
        total = dot(high, y_back_ref[0]) + dot(low, y_back_ref[0]) + dot(high, y_back_ref[1])
        for band in range(bands):
            boxes[plane, pl.ds(band, blocks, stride=bands), :] = total[
                band * blocks : (band + 1) * blocks, :
            ]
        return carry

    lax.fori_loop(0, planes, transform, 0)

    first_product = blocks - 2 * products.shape[0]
    for pair in range(products.shape[0]):
        for plane in range(0, planes, 2):
            sides = []
            for block in (first_product + 2 * pair, first_product + 2 * pair + 1):
                cut = slice(block * bands, (block + 1) * bands)
                sides.append(jnp.concatenate([boxes[plane, cut, :], boxes[plane + 1, cut, :]], axis=0))
            high, low = split(jnp.concatenate(sides, axis=1))
            products[pair, plane * bands : (plane + 2) * bands, :] = high
            products[pair, (planes + plane) * bands : (planes + plane + 2) * bands, :] = low
    lane_rows = lax.broadcasted_iota(jnp.int32, (2 * LANES, 2 * LANES), 0)

    def pick(pair, carry):
        places = [box_ref[pl.ds(pair * 2 + side, 1), :] for side in range(2)]
        wide = jnp.concatenate(places, axis=1)
        rest = jnp.zeros((2 * planes * bands, 2 * LANES), F32)
        for step in range(products.shape[0]):
            low = (first_product + 2 * step) * LANES
            rest = rest + dot(products[step], (wide - low == lane_rows).astype(F32).astype(BF16))
        rest = rest[: planes * bands] + rest[planes * bands :]
        for side in range(2):
            place = jnp.broadcast_to(places[side], (bands, LANES))
            lane_of = place & (LANES - 1)
            block_of = lax.shift_right_logical(place, 7)
            values = [jnp.zeros((bands, LANES), F32) for _ in range(planes)]
            for block in range(first_product):
                here = block_of == block
                for plane in range(planes):
                    values[plane] = jnp.where(
                        here,
                        take_lanes(boxes[plane, block * bands : (block + 1) * bands, :], lane_of),
                        values[plane],
                    )
            for plane in range(planes):
                cut = slice(plane * bands, (plane + 1) * bands)
                staged[pair * 2 + side, plane] = (
                    values[plane] + rest[cut, side * LANES : (side + 1) * LANES]
                )
        return carry

    lax.fori_loop(0, sources // 2, pick, 0)
    for source, plane, core, row in places:
        out_ref[row : row + HALF, :] = staged[source, plane, core * HALF : (core + 1) * HALF]


def backward_kernel(
    grid_cells, rows, starts, packet_ref, own_ref, cas_ref, returned_ref, out_ref, dense, packed, slots
):
    z_transform(cas_ref, returned_ref, dense, grid_cells)
    slots[...] = jnp.full(slots.shape, -1, jnp.int32)
    for block in range(BLOCKS):
        first = block * ROWS + SLOT_ROW
        slots[block, :rows] = packet_ref[first : first + rows, :].astype(jnp.int32)
    packed[...] = jnp.zeros_like(packed)

    def for_bands(rows_of):
        return jnp.concatenate([jnp.broadcast_to(row, (HALF, LANES)) for row in rows_of], axis=0)

    def compact(height, carry):
        values = dense[pl.ds(pl.multiple_of(height * GANG, GANG), GANG), :]
        for step in range(2):
            near = [
                lax.shift_right_logical(starts[block, height], 7) + step for block in range(BLOCKS)
            ]
            cuts = [pl.ds(pl.multiple_of(row * HALF, HALF), HALF) for row in near]
            own = for_bands([slots[block, pl.ds(near[block], 1), :] for block in range(BLOCKS)])
            old = jnp.concatenate([packed[block, cuts[block], :] for block in range(BLOCKS)], axis=0)
            mask = lax.shift_right_logical(own, 7) == height
            new = jnp.where(mask, take_lanes(values, own & (LANES - 1)), old)
            for block in range(BLOCKS):
                packed[block, cuts[block], :] = new[block * HALF : (block + 1) * HALF, :]
        return carry

    lax.fori_loop(0, grid_cells, compact, 0, unroll=8)
    first, second = column_box(own_ref[...], grid_cells)
    radial = (first * first + second * second).astype(F32)
    radial = for_bands([radial[block : block + 1, :] for block in range(BLOCKS)])
    parts = out_ref.shape[0] // (SIZES[1] * GANG * 8)
    each = -(-rows // parts)
    for part in range(parts):
        for place in range(8):
            row = part * each + place
            if place >= each or row >= rows:
                value = jnp.zeros((GANG, LANES), F32)
            else:
                own = for_bands([slots[block, row : row + 1, :] for block in range(BLOCKS)])
                height = wrapped(lax.shift_right_logical(own, 7), grid_cells)
                around = take_lanes(radial, own & (LANES - 1))
                kinetic = 2.0 * (around + (height * height).astype(F32)) / (K * K)
                cut = slice(row * HALF, (row + 1) * HALF)
                trial = jnp.concatenate(
                    [packet_ref[block * ROWS + cut.start : block * ROWS + cut.stop, :] for block in range(BLOCKS)],
                    axis=0,
                )
                value = jnp.concatenate([packed[block, cut, :] for block in range(BLOCKS)], axis=0)
                value = value + kinetic * trial
            for zh in range(SIZES[1]):
                to = (part // SIZES[2] * SIZES[1] + zh) * SIZES[2] + part % SIZES[2]
                out_ref[pl.ds(to * GANG * 8 + place, GANG, stride=8), :] = value


def constant_tables(grid_cells):
    fine = 2 * K
    order = np.arange(grid_cells).reshape(SIZES[3], SIZES[2], SIZES[5], -1)
    order = order.transpose(1, 0, 2, 3).reshape(-1)
    high, low = halves(cas_matrix(grid_cells))
    cas_out = np.concatenate([high[order], high[order], low[order]], axis=1)
    cas_back = np.concatenate([high[:, order], high[:, order], low[:, order]], axis=1)
    theta = (np.arange(fine) + 0.5) / fine
    full = np.arange(grid_cells) / grid_cells
    box = np.arange(K) - K // 2
    angle = 2.0 * math.pi * box[:, None] * theta[None, :]
    box_table = ((np.cos(angle) + np.sin(angle)) / math.sqrt(fine)).astype(np.float32)
    waves = 2.0 * math.pi * np.arange(1, K)
    apart = theta[:, None] - full[None, :]
    project = 1.0 + 2.0 * np.cos(waves[:, None, None] * apart[None]).sum(axis=0)
    edge = 2.0 * math.pi * K
    project = project + np.sin(edge * theta)[:, None] * np.sin(edge * full)[None, :]
    project = (project / grid_cells).astype(np.float32)
    high, low = halves(project)
    filter_three = np.concatenate([high, high, low], axis=1)
    filter_back = np.stack([high.T, low.T])
    sides = np.zeros((2, K, 2, fine), np.float32)
    for side in range(2):
        sides[side, :, side, :] = box_table
    high, low = halves(sides.reshape(2 * K, 2 * fine))
    y_three = np.concatenate([high, high, low], axis=0)
    y_back = np.stack([high.T, low.T])
    order = np.concatenate([np.arange(0, K, 2), np.arange(1, K, 2)])
    high, low = halves(box_table[order])
    x_three = np.concatenate([high, high, low], axis=0).T
    x_back = np.concatenate([high, low], axis=0)
    tables = (cas_out, cas_back, filter_three, filter_back, y_three, x_three, x_back, y_back)
    return tuple(jnp.asarray(one) for one in tables)


def swap_pairs(turn):
    place = np.arange(math.prod(SIZES)).reshape(SIZES)
    pairs = []
    for (y, zh, c, x, l2, ll), target in np.ndenumerate(place):
        near = zh if l2 == c else (zh * 2 + l2 + turn) % 4 // 2
        pairs.append((int(place[y, near, l2, x, c, ll]), int(target)))
    return tuple(pairs)


def swapped(block, axis):
    return lax.ppermute(block, axis, ((0, 1), (1, 0)))


def arrange(block):
    parts = lax.axis_size(SIDE)
    width = -(-block.shape[1] // (LANES * parts)) * LANES
    block = jnp.pad(block, ((0, 0), (0, parts * width - block.shape[1])))
    return block.reshape(-1, parts, width).transpose(1, 0, 2)


def apply_hamiltonian(trial_block, potential, positions, sphere_slots, all_bands):
    bands, coefs = trial_block.shape
    planes, grid_cells = potential.shape[:2]
    fft_size = lax.axis_size(FFT)
    rows = coefs // LANES
    slots = sphere_slots.reshape(rows, LANES)
    position_rows = positions.reshape(fft_size, LANES)
    own = position_rows.reshape(SIZES[3], BLOCKS, SIZES[5], LANES)
    own = lax.dynamic_index_in_dim(own, lax.axis_index("x"), 0, keepdims=False)
    own = lax.dynamic_index_in_dim(own, lax.axis_index("ll"), 1, keepdims=False)
    cas_out, cas_back, filter_three, filter_back, *plane_tables = constant_tables(grid_cells)
    i32 = functools.partial(jax.ShapeDtypeStruct, dtype=jnp.int32)
    f32 = functools.partial(jax.ShapeDtypeStruct, dtype=F32)
    params = pltpu.CompilerParams(vmem_limit_bytes=48 * 2**20)
    smem = pl.BlockSpec(memory_space=pltpu.SMEM)
    vmem = pl.BlockSpec(memory_space=pltpu.VMEM)
    half = lax.axis_index("l2")
    packet = f32((ROWS, LANES))
    kept, sent = pl.pallas_call(
        functools.partial(pack_kernel, grid_cells),
        out_shape=(packet, packet),
        in_specs=[smem] + [vmem] * 2,
        out_specs=[vmem] * 2,
        compiler_params=params,
        name="pack",
    )(half.reshape(1), slots, trial_block)
    sent, potential, pieces, position_rows = lax.optimization_barrier(
        (sent, potential, all_bands, position_rows)
    )
    other = swapped(sent, "l2")
    pieces = arrange(jnp.concatenate([pieces, trial_block], axis=0))
    inverse, box = pl.pallas_call(
        functools.partial(boxes_kernel, grid_cells),
        out_shape=(i32((2 * fft_size, LANES)), i32((fft_size, LANES))),
        compiler_params=params,
        name="boxes",
    )(position_rows)
    filtered = pl.pallas_call(
        potential_kernel,
        out_shape=f32((planes, 2 * K, 2 * K)),
        compiler_params=params,
        name="filter",
    )(filter_three, filter_back, potential)
    cut = planes // 2
    filtered = [
        lax.ppermute(part, BAND + FFT, swap_pairs(turn))
        for part, turn in ((filtered[:cut], 1), (filtered[cut:], -1))
    ]
    packet = jnp.where(half == 0, jnp.stack([kept, other]), jnp.stack([other, kept]))
    starts = packet[:, START_ROW : START_ROW + 2].reshape(BLOCKS, -1).astype(jnp.int32)
    packet = packet.reshape(BLOCKS * ROWS, LANES)
    dense_rows = grid_cells * GANG
    dense = pltpu.VMEM((dense_rows, LANES), F32)
    mixed = pl.pallas_call(
        functools.partial(forward_kernel, grid_cells),
        out_shape=f32((dense_rows, LANES)),
        in_specs=[smem, vmem, vmem],
        out_specs=vmem,
        scratch_shapes=[pltpu.VMEM((dense_rows, LANES), jnp.int32), dense],
        compiler_params=params,
        name="forward",
    )(starts, packet, cas_out)
    filtered = jnp.concatenate(filtered, axis=0)
    pieces = lax.all_to_all(pieces, SIDE, 0, 0, tiled=True)
    mixed, filtered, pieces = lax.optimization_barrier((mixed, filtered, pieces))
    gathered = lax.all_to_all(mixed, GROUP, 0, 0, tiled=True)
    trial = pieces[:, -bands:].reshape(-1, pieces.shape[2])
    gathered, trial = lax.optimization_barrier((gathered, trial))
    theirs = swapped(trial, "zh")
    weighted = pl.pallas_call(
        plane_kernel,
        out_shape=f32(gathered.shape),
        scratch_shapes=[
            pltpu.VMEM((planes, fft_size * bands, LANES), F32),
            pltpu.VMEM((fft_size, planes, bands, LANES), F32),
            pltpu.VMEM((8, 2 * planes * bands, 2 * LANES), BF16),
        ],
        compiler_params=params,
        cost_estimate=pl.CostEstimate(
            flops=25 * 10**9, bytes_accessed=60 * 10**6, transcendentals=0
        ),
        name="planes",
    )(inverse, box, *plane_tables, filtered, gathered)
    weighted, theirs = lax.optimization_barrier((weighted, theirs))
    returned = lax.all_to_all(weighted, GROUP, 0, 0, tiled=True)
    parts = pieces.shape[0]
    tall = rows + 7 & -8
    applied = pl.pallas_call(
        functools.partial(backward_kernel, grid_cells, rows),
        out_shape=f32((SIZES[1] * parts * GANG * 8, LANES)),
        in_specs=[smem] + [vmem] * 4,
        out_specs=vmem,
        scratch_shapes=[
            dense,
            pltpu.VMEM((BLOCKS, tall * HALF, LANES), F32),
            pltpu.VMEM((BLOCKS, tall, LANES), jnp.int32),
        ],
        compiler_params=params,
        cost_estimate=pl.CostEstimate(flops=8 * 10**9, bytes_accessed=16 * 10**6, transcendentals=0),
        name="backward",
    )(starts, packet, own, cas_back, returned)
    applied = lax.all_to_all(applied, BAND + ("l2",), 0, 0, tiled=True)
    each = pieces.shape[2] // LANES
    applied = applied.reshape(-1, 8, LANES)[:, :each].reshape(2 * trial.shape[0], -1)
    return applied, pieces[:, :-bands], jnp.concatenate([trial, theirs], axis=0)


def per_device(trial_block, all_bands, potential, positions, sphere_slots):
    applied, pieces, trial = apply_hamiltonian(
        trial_block, potential, positions, sphere_slots, all_bands
    )
    pieces = pieces.reshape(-1, pieces.shape[2])
    products = [
        jnp.einsum("ag,bg->ab", pieces, block, precision=lax.Precision.HIGH)
        for block in (trial, applied)
    ]
    products = jnp.concatenate(products, axis=1)
    columns = products.shape[1]
    near = lax.all_to_all(products, NEAR, 0, 0, tiled=True)
    near = jnp.sum(near.reshape(lax.axis_size(NEAR), -1, columns), axis=0)
    far = lax.all_to_all(near, ("l2", "ll"), 0, 0, tiled=True)
    total = jnp.sum(far, axis=0).reshape(2, -1)
    first = total[0].reshape(SIZES[1], SIZES[0], SIZES[2], -1)
    first = jnp.where(lax.axis_index("zh") == 0, first, first[::-1]).transpose(1, 0, 2, 3)
    return (first.reshape(1, -1), total[1:])


def solution(mesh):
    axes = Mesh(mesh.devices.reshape(SIZES), AXES)
    placed = (P(BAND, FFT), P(BAND, FFT), P(FFT, None, None), P(), P(FFT))
    return jax.shard_map(
        per_device,
        mesh=axes,
        in_specs=placed,
        out_specs=(P(BAND + FFT, None), P(BAND + FFT, None)),
        check_vma=False,
    )
```

```python
import functools
import math

import jax
import jax.numpy as jnp
import numpy as np
from jax import lax
from jax.experimental import pallas as pl
from jax.experimental.pallas import tpu as pltpu
from jax.sharding import Mesh
from jax.sharding import PartitionSpec as P

K = 64
LANES = 128
SIZES = (4, 2, 2, 4, 2, 4)
AXES = ("y", "zh", "c", "x", "l2", "ll")
BAND = ("y", "zh", "c")
FFT = ("x", "l2", "ll")
SIDE = ("y", "c")
NEAR = ("y", "c", "x")
GROUP = ("c", "x", "ll")
BLOCKS = 2
HALF = 4
GANG = BLOCKS * HALF
REACH_ROW, START_ROW, SLOT_ROW, ROWS = 196, 200, 204, 256
F32 = jnp.float32
BF16 = jnp.bfloat16


def cas_matrix(length):
    ids = np.arange(length)
    angle = (ids[:, None] * ids[None, :] % length) * (2.0 * math.pi / length)
    return ((np.cos(angle) + np.sin(angle)) / math.sqrt(length)).astype(np.float32)


def halves(table):
    high = table.astype(jnp.bfloat16)
    low = (table - high.astype(np.float32)).astype(jnp.bfloat16)
    return high, low


def split(values):
    high = values.astype(BF16)
    low = (values - high.astype(F32)).astype(BF16)
    return high, low


def dot(left, right):
    return jnp.dot(left, right, preferred_element_type=F32)


def wrapped(values, length):
    return jnp.where(values >= length // 2, values - length, values)


def take_lanes(row, lanes):
    return jnp.take_along_axis(row, lanes, axis=1, mode="promise_in_bounds")


def column_box(positions, grid_cells):
    first = lax.shift_right_logical(lax.shift_right_logical(positions, 6) * 43691, 17)
    second = positions - first * grid_cells
    return wrapped(first, grid_cells), wrapped(second, grid_cells)


def upper(size):
    ids = [lax.broadcasted_iota(jnp.int32, (size, size), axis) for axis in range(2)]
    return (ids[0] < ids[1]).astype(BF16)


def nt_dot(left, right):
    return lax.dot_general(left, right, (((1,), (1,)), ((), ())), preferred_element_type=F32)


def pack_kernel(
    grid_cells, half, slots_ref, trial_ref, own_ref, send_ref
):
    rows = slots_ref.shape[0]
    first_half = half[0] == 0
    column = slots_ref[...] & (LANES - 1)
    lane_ids = lax.broadcasted_iota(jnp.int32, (LANES, LANES), 0)
    ones = jnp.ones((8, LANES), BF16)
    total = jnp.zeros((8, LANES), F32)
    for row in range(rows):
        hit = (column[row : row + 1, :] == lane_ids).astype(BF16)
        total = total + nt_dot(ones, hit)
    reach = (total - 1.0) * 0.5
    padded = 2 * LANES
    height = lax.broadcasted_iota(jnp.int32, (padded, LANES), 0)
    away = jnp.abs(wrapped(height, grid_cells)).astype(F32)
    valid = ((away <= reach[0:1, :]) & (height < grid_cells)).astype(BF16)
    start = dot(nt_dot(ones, valid).astype(BF16), upper(padded))
    for row in range(rows):
        values = trial_ref[:, row * LANES : (row + 1) * LANES]
        own_ref[row * HALF : (row + 1) * HALF, :] = jnp.where(
            first_half, values[:HALF], values[HALF:]
        )
        send_ref[row * HALF : (row + 1) * HALF, :] = jnp.where(
            first_half, values[HALF:], values[:HALF]
        )
    own_slots = slots_ref[...].astype(F32)
    for packet_ref in (own_ref, send_ref):
        packet_ref[REACH_ROW : REACH_ROW + HALF, :] = reach[:HALF]
        packet_ref[START_ROW : START_ROW + 1, :] = start[:1, :LANES]
        packet_ref[START_ROW + 1 : START_ROW + 2, :] = start[:1, LANES:]
        packet_ref[START_ROW + 2 : SLOT_ROW, :] = jnp.zeros((2, LANES), F32)
        packet_ref[SLOT_ROW : SLOT_ROW + rows, :] = own_slots
        packet_ref[SLOT_ROW + rows :, :] = jnp.zeros((ROWS - SLOT_ROW - rows, LANES), F32)


def boxes_kernel(grid_cells, positions_ref, inverse_ref, box_ref):
    lane_ids = lax.broadcasted_iota(jnp.int32, (LANES, LANES), 0)
    first, second = column_box(positions_ref[...], grid_cells)
    box = (first + K // 2) * K + second + K // 2
    box_ref[...] = box
    sources = positions_ref.shape[0]
    blocks = sources
    block_ids = lax.broadcasted_iota(jnp.int32, (blocks, LANES), 0)
    own_lane = lax.broadcasted_iota(jnp.int32, (blocks, LANES), 1).astype(F32)
    inverse = jnp.zeros((2 * blocks, LANES), F32)
    for source in range(sources):
        place = box[source : source + 1, :]
        in_block = lax.shift_right_logical(place, 7) == block_ids
        left = jnp.concatenate(
            [jnp.where(in_block, float(source), 0.0), jnp.where(in_block, own_lane, 0.0)], axis=0
        ).astype(BF16)
        right = ((place & (LANES - 1)) == lane_ids).astype(BF16)
        inverse = inverse + nt_dot(left, right)
    inverse_ref[...] = inverse.astype(jnp.int32)


def z_transform(cas_ref, source_ref, out_ref, grid_cells):
    for block in range(0, GANG, 2):
        pair = jnp.concatenate(
            [source_ref[pl.ds(block + side, grid_cells, stride=GANG), :] for side in range(2)],
            axis=1,
        )
        high, low = split(pair)
        mixed = dot(cas_ref[...], jnp.concatenate([high, low, high], axis=0))
        for side in range(2):
            out_ref[pl.ds(block + side, grid_cells, stride=GANG), :] = mixed[
                :, side * LANES : (side + 1) * LANES
            ]


def forward_kernel(grid_cells, starts, packet_ref, cas_ref, out_ref, places, dense):
    height = lax.broadcasted_iota(jnp.int32, (grid_cells, LANES), 0)
    away = jnp.abs(wrapped(height, grid_cells)).astype(F32)
    ids = [lax.broadcasted_iota(jnp.int32, (grid_cells, grid_cells), axis) for axis in range(2)]
    below = (ids[0] > ids[1]).astype(BF16)
    before = upper(LANES)
    every = jnp.ones((LANES, LANES), BF16)
    for block in range(BLOCKS):
        row = block * ROWS + REACH_ROW
        valid = away <= packet_ref[row : row + 1, :]
        valid_one = valid.astype(BF16)
        rank = dot(valid_one, before).astype(jnp.int32)
        start = dot(below, dot(valid_one, every).astype(BF16)).astype(jnp.int32)
        place = jnp.where(valid, rank + (start & (LANES - 1)), -1)
        for band in range(HALF):
            places[pl.ds(block * HALF + band, grid_cells, stride=GANG), :] = place

    def expand(height, carry):
        rows = [
            block * ROWS + lax.shift_right_logical(starts[block, height], 7) * HALF
            for block in range(BLOCKS)
        ]
        rows = [pl.multiple_of(row, HALF) for row in rows]
        here = jnp.concatenate([packet_ref[pl.ds(row, HALF), :] for row in rows], axis=0)
        there = jnp.concatenate([packet_ref[pl.ds(row + HALF, HALF), :] for row in rows], axis=0)
        cut = pl.ds(pl.multiple_of(height * GANG, GANG), GANG)
        place = places[cut, :]
        lanes = place & (LANES - 1)
        value = jnp.where(place < LANES, take_lanes(here, lanes), take_lanes(there, lanes))
        dense[cut, :] = jnp.where(place < 0, 0.0, value)
        return carry

    lax.fori_loop(0, grid_cells, expand, 0, unroll=8)
    z_transform(cas_ref, dense, out_ref, grid_cells)


def potential_kernel(filter_ref, filter_t_ref, potential_ref, out_ref):
    for plane in range(potential_ref.shape[0]):
        high, low = split(potential_ref[plane])
        rows = dot(filter_ref[...], jnp.concatenate([high, low, high], axis=0))
        high, low = split(rows)
        out_ref[plane] = (
            dot(high, filter_t_ref[0]) + dot(low, filter_t_ref[0]) + dot(high, filter_t_ref[1])
        )


def plane_kernel(
    inverse_ref,
    box_ref,
    y_ref,
    x_ref,
    x_back_ref,
    y_back_ref,
    potential_ref,
    columns_ref,
    out_ref,
    boxes,
    staged,
    products,
):
    sources, planes, bands = staged.shape[:3]
    blocks = sources
    cores, runs = bands // HALF, SIZES[5]
    places = [
        (source, plane, core, (((core * SIZES[3] + x) * runs + run) * planes + plane) * GANG + block * HALF)
        for source, (x, block, run) in enumerate(np.ndindex(SIZES[3], BLOCKS, runs))
        for plane in range(planes)
        for core in range(cores)
    ]
    for source, plane, core, row in places:
        staged[source, plane, core * HALF : (core + 1) * HALF] = columns_ref[row : row + HALF, :]

    steps = products.shape[0]
    first_product = blocks - 2 * steps
    lane_rows = lax.broadcasted_iota(jnp.int32, (2 * LANES, 2 * LANES), 0)

    def stage_products(piece):
        for step in range(steps):
            for plane in range(0, planes, 2):
                sides = [
                    jnp.concatenate([piece(plane, at), piece(plane + 1, at)], axis=0)
                    for at in (first_product + 2 * step, first_product + 2 * step + 1)
                ]
                high, low = split(jnp.concatenate(sides, axis=1))
                products[step, plane * bands : (plane + 2) * bands, :] = high
                products[step, (planes + plane) * bands : (planes + plane + 2) * bands, :] = low

    def one_hot_part(wide):
        rest = jnp.zeros((2 * planes * bands, 2 * LANES), F32)
        for step in range(steps):
            low = (first_product + 2 * step) * LANES
            rest = rest + dot(products[step], (wide - low == lane_rows).astype(F32).astype(BF16))
        return rest[: planes * bands] + rest[planes * bands :]

    def gather_part(piece, from_of, lane_of):
        values = [jnp.zeros((bands, LANES), F32) for _ in range(planes)]
        for at in range(first_product):
            here = from_of == at
            for plane in range(planes):
                values[plane] = jnp.where(here, take_lanes(piece(plane, at), lane_of), values[plane])
        return values

    def column_piece(plane, source):
        return staged[source, plane]

    def box_piece(plane, block):
        return boxes[plane, block * bands : (block + 1) * bands, :]

    stage_products(column_piece)

    def fill(pair, carry):
        from_rows = [inverse_ref[pl.ds(pair * 2 + side, 1), :] for side in range(2)]
        lane_rows_of = [inverse_ref[pl.ds(pair * 2 + side + blocks, 1), :] for side in range(2)]
        wide = [from_rows[side] * LANES + lane_rows_of[side] for side in range(2)]
        rest = one_hot_part(jnp.concatenate(wide, axis=1))
        for side in range(2):
            from_of = jnp.broadcast_to(from_rows[side], (bands, LANES))
            lane_of = jnp.broadcast_to(lane_rows_of[side], (bands, LANES))
            values = gather_part(column_piece, from_of, lane_of)
            goal = pl.ds(pl.multiple_of((pair * 2 + side) * bands, bands), bands)
            for plane in range(planes):
                cut = slice(plane * bands, (plane + 1) * bands)
                boxes[plane, goal, :] = (
                    values[plane] + rest[cut, side * LANES : (side + 1) * LANES]
                )
        return carry

    lax.fori_loop(0, blocks // 2, fill, 0)

    def transform(plane, carry):
        stacked = jnp.concatenate(
            [boxes[plane, pl.ds(band, blocks, stride=bands), :] for band in range(bands)], axis=0
        )
        high, low = split(stacked)
        wide = dot(jnp.concatenate([high, low, high], axis=1), y_ref[...])
        potential = potential_ref[plane]
        potential = jnp.concatenate([potential, potential], axis=1)
        back = []
        for band in range(0, bands, 2):
            pair = []
            for one in (band, band + 1):
                mine = wide[one * blocks : (one + 1) * blocks, :]
                pair.append(jnp.concatenate([mine[:, :LANES], mine[:, LANES:]], axis=0))
            high, low = split(jnp.concatenate(pair, axis=1))
            field = dot(x_ref[...], jnp.concatenate([high, low, high], axis=0))
            high, low = split(field * potential)
            both = dot(x_back_ref[...], high)
            both = both[:K] + both[K:] + dot(x_back_ref[:K, :], low)
            for side in range(2):
                one = both[:, side * LANES : (side + 1) * LANES]
                back.append(jnp.concatenate([one[:blocks], one[blocks:]], axis=1))
        high, low = split(jnp.concatenate(back, axis=0))
        total = dot(high, y_back_ref[0]) + dot(low, y_back_ref[0]) + dot(high, y_back_ref[1])
        for band in range(bands):
            boxes[plane, pl.ds(band, blocks, stride=bands), :] = total[
                band * blocks : (band + 1) * blocks, :
            ]
        return carry

    lax.fori_loop(0, planes, transform, 0)

    stage_products(box_piece)

    def pick(pair, carry):
        places = [box_ref[pl.ds(pair * 2 + side, 1), :] for side in range(2)]
        rest = one_hot_part(jnp.concatenate(places, axis=1))
        for side in range(2):
            place = jnp.broadcast_to(places[side], (bands, LANES))
            values = gather_part(
                box_piece, lax.shift_right_logical(place, 7), place & (LANES - 1)
            )
            for plane in range(planes):
                cut = slice(plane * bands, (plane + 1) * bands)
                staged[pair * 2 + side, plane] = (
                    values[plane] + rest[cut, side * LANES : (side + 1) * LANES]
                )
        return carry

    lax.fori_loop(0, sources // 2, pick, 0)
    for source, plane, core, row in places:
        out_ref[row : row + HALF, :] = staged[source, plane, core * HALF : (core + 1) * HALF]


def backward_kernel(
    grid_cells, rows, starts, packet_ref, own_ref, cas_ref, returned_ref, out_ref, dense, packed, slots
):
    z_transform(cas_ref, returned_ref, dense, grid_cells)
    slots[...] = jnp.full(slots.shape, -1, jnp.int32)
    for block in range(BLOCKS):
        first = block * ROWS + SLOT_ROW
        slots[block, :rows] = packet_ref[first : first + rows, :].astype(jnp.int32)
    packed[...] = jnp.zeros_like(packed)

    def for_bands(rows_of):
        return jnp.concatenate([jnp.broadcast_to(row, (HALF, LANES)) for row in rows_of], axis=0)

    def compact(height, carry):
        values = dense[pl.ds(pl.multiple_of(height * GANG, GANG), GANG), :]
        for step in range(2):
            near = [
                lax.shift_right_logical(starts[block, height], 7) + step for block in range(BLOCKS)
            ]
            cuts = [pl.ds(pl.multiple_of(row * HALF, HALF), HALF) for row in near]
            own = for_bands([slots[block, pl.ds(near[block], 1), :] for block in range(BLOCKS)])
            old = jnp.concatenate([packed[block, cuts[block], :] for block in range(BLOCKS)], axis=0)
            mask = lax.shift_right_logical(own, 7) == height
            new = jnp.where(mask, take_lanes(values, own & (LANES - 1)), old)
            for block in range(BLOCKS):
                packed[block, cuts[block], :] = new[block * HALF : (block + 1) * HALF, :]
        return carry

    lax.fori_loop(0, grid_cells, compact, 0, unroll=8)
    first, second = column_box(own_ref[...], grid_cells)
    radial = (first * first + second * second).astype(F32)
    radial = for_bands([radial[block : block + 1, :] for block in range(BLOCKS)])
    parts = out_ref.shape[0] // (SIZES[1] * GANG * 8)
    each = -(-rows // parts)
    for part in range(parts):
        for place in range(8):
            row = part * each + place
            if place >= each or row >= rows:
                value = jnp.zeros((GANG, LANES), F32)
            else:
                own = for_bands([slots[block, row : row + 1, :] for block in range(BLOCKS)])
                height = wrapped(lax.shift_right_logical(own, 7), grid_cells)
                around = take_lanes(radial, own & (LANES - 1))
                kinetic = 2.0 * (around + (height * height).astype(F32)) / (K * K)
                cut = slice(row * HALF, (row + 1) * HALF)
                trial = jnp.concatenate(
                    [packet_ref[block * ROWS + cut.start : block * ROWS + cut.stop, :] for block in range(BLOCKS)],
                    axis=0,
                )
                value = jnp.concatenate([packed[block, cut, :] for block in range(BLOCKS)], axis=0)
                value = value + kinetic * trial
            for zh in range(SIZES[1]):
                to = (part // SIZES[2] * SIZES[1] + zh) * SIZES[2] + part % SIZES[2]
                out_ref[pl.ds(to * GANG * 8 + place, GANG, stride=8), :] = value


def constant_tables(grid_cells):
    fine = 2 * K
    order = np.arange(grid_cells).reshape(SIZES[3], SIZES[2], SIZES[5], -1)
    order = order.transpose(1, 0, 2, 3).reshape(-1)
    high, low = halves(cas_matrix(grid_cells))
    cas_out = np.concatenate([high[order], high[order], low[order]], axis=1)
    cas_back = np.concatenate([high[:, order], high[:, order], low[:, order]], axis=1)
    theta = (np.arange(fine) + 0.5) / fine
    full = np.arange(grid_cells) / grid_cells
    box = np.arange(K) - K // 2
    angle = 2.0 * math.pi * box[:, None] * theta[None, :]
    box_table = ((np.cos(angle) + np.sin(angle)) / math.sqrt(fine)).astype(np.float32)
    waves = 2.0 * math.pi * np.arange(1, K)
    apart = theta[:, None] - full[None, :]
    project = 1.0 + 2.0 * np.cos(waves[:, None, None] * apart[None]).sum(axis=0)
    edge = 2.0 * math.pi * K
    project = project + np.sin(edge * theta)[:, None] * np.sin(edge * full)[None, :]
    project = (project / grid_cells).astype(np.float32)
    high, low = halves(project)
    filter_three = np.concatenate([high, high, low], axis=1)
    filter_back = np.stack([high.T, low.T])
    sides = np.zeros((2, K, 2, fine), np.float32)
    for side in range(2):
        sides[side, :, side, :] = box_table
    high, low = halves(sides.reshape(2 * K, 2 * fine))
    y_three = np.concatenate([high, high, low], axis=0)
    y_back = np.stack([high.T, low.T])
    order = np.concatenate([np.arange(0, K, 2), np.arange(1, K, 2)])
    high, low = halves(box_table[order])
    x_three = np.concatenate([high, high, low], axis=0).T
    x_back = np.concatenate([high, low], axis=0)
    tables = (cas_out, cas_back, filter_three, filter_back, y_three, x_three, x_back, y_back)
    return tuple(jnp.asarray(one) for one in tables)


def swap_pairs(turn):
    place = np.arange(math.prod(SIZES)).reshape(SIZES)
    pairs = []
    for (y, zh, c, x, l2, ll), target in np.ndenumerate(place):
        near = zh if l2 == c else (zh * 2 + l2 + turn) % 4 // 2
        pairs.append((int(place[y, near, l2, x, c, ll]), int(target)))
    return tuple(pairs)


def swapped(block, axis):
    return lax.ppermute(block, axis, ((0, 1), (1, 0)))


def arrange(block):
    parts = lax.axis_size(SIDE)
    width = -(-block.shape[1] // (LANES * parts)) * LANES
    block = jnp.pad(block, ((0, 0), (0, parts * width - block.shape[1])))
    return block.reshape(-1, parts, width).transpose(1, 0, 2)


def apply_hamiltonian(trial_block, potential, positions, sphere_slots, all_bands):
    bands, coefs = trial_block.shape
    planes, grid_cells = potential.shape[:2]
    fft_size = lax.axis_size(FFT)
    rows = coefs // LANES
    slots = sphere_slots.reshape(rows, LANES)
    position_rows = positions.reshape(fft_size, LANES)
    own = position_rows.reshape(SIZES[3], BLOCKS, SIZES[5], LANES)
    own = lax.dynamic_index_in_dim(own, lax.axis_index("x"), 0, keepdims=False)
    own = lax.dynamic_index_in_dim(own, lax.axis_index("ll"), 1, keepdims=False)
    cas_out, cas_back, filter_three, filter_back, *plane_tables = constant_tables(grid_cells)
    i32 = functools.partial(jax.ShapeDtypeStruct, dtype=jnp.int32)
    f32 = functools.partial(jax.ShapeDtypeStruct, dtype=F32)
    params = pltpu.CompilerParams(vmem_limit_bytes=48 * 2**20)
    smem = pl.BlockSpec(memory_space=pltpu.SMEM)
    vmem = pl.BlockSpec(memory_space=pltpu.VMEM)
    half = lax.axis_index("l2")
    packet = f32((ROWS, LANES))
    kept, sent = pl.pallas_call(
        functools.partial(pack_kernel, grid_cells),
        out_shape=(packet, packet),
        in_specs=[smem] + [vmem] * 2,
        out_specs=[vmem] * 2,
        compiler_params=params,
        name="pack",
    )(half.reshape(1), slots, trial_block)
    sent, potential, pieces, position_rows = lax.optimization_barrier(
        (sent, potential, all_bands, position_rows)
    )
    other = swapped(sent, "l2")
    pieces = arrange(jnp.concatenate([pieces, trial_block], axis=0))
    inverse, box = pl.pallas_call(
        functools.partial(boxes_kernel, grid_cells),
        out_shape=(i32((2 * fft_size, LANES)), i32((fft_size, LANES))),
        compiler_params=params,
        name="boxes",
    )(position_rows)
    filtered = pl.pallas_call(
        potential_kernel,
        out_shape=f32((planes, 2 * K, 2 * K)),
        compiler_params=params,
        name="filter",
    )(filter_three, filter_back, potential)
    cut = planes // 2
    filtered = [
        lax.ppermute(part, BAND + FFT, swap_pairs(turn))
        for part, turn in ((filtered[:cut], 1), (filtered[cut:], -1))
    ]
    packet = jnp.where(half == 0, jnp.stack([kept, other]), jnp.stack([other, kept]))
    starts = packet[:, START_ROW : START_ROW + 2].reshape(BLOCKS, -1).astype(jnp.int32)
    packet = packet.reshape(BLOCKS * ROWS, LANES)
    dense_rows = grid_cells * GANG
    dense = pltpu.VMEM((dense_rows, LANES), F32)
    mixed = pl.pallas_call(
        functools.partial(forward_kernel, grid_cells),
        out_shape=f32((dense_rows, LANES)),
        in_specs=[smem, vmem, vmem],
        out_specs=vmem,
        scratch_shapes=[pltpu.VMEM((dense_rows, LANES), jnp.int32), dense],
        compiler_params=params,
        name="forward",
    )(starts, packet, cas_out)
    filtered = jnp.concatenate(filtered, axis=0)
    pieces = lax.all_to_all(pieces, SIDE, 0, 0, tiled=True)
    mixed, filtered, pieces = lax.optimization_barrier((mixed, filtered, pieces))
    gathered = lax.all_to_all(mixed, GROUP, 0, 0, tiled=True)
    trial = pieces[:, -bands:].reshape(-1, pieces.shape[2])
    gathered, trial = lax.optimization_barrier((gathered, trial))
    theirs = swapped(trial, "zh")
    weighted = pl.pallas_call(
        plane_kernel,
        out_shape=f32(gathered.shape),
        scratch_shapes=[
            pltpu.VMEM((planes, fft_size * bands, LANES), F32),
            pltpu.VMEM((fft_size, planes, bands, LANES), F32),
            pltpu.VMEM((8, 2 * planes * bands, 2 * LANES), BF16),
        ],
        compiler_params=params,
        cost_estimate=pl.CostEstimate(
            flops=25 * 10**9, bytes_accessed=60 * 10**6, transcendentals=0
        ),
        name="planes",
    )(inverse, box, *plane_tables, filtered, gathered)
    weighted, theirs = lax.optimization_barrier((weighted, theirs))
    returned = lax.all_to_all(weighted, GROUP, 0, 0, tiled=True)
    parts = pieces.shape[0]
    tall = rows + 7 & -8
    applied = pl.pallas_call(
        functools.partial(backward_kernel, grid_cells, rows),
        out_shape=f32((SIZES[1] * parts * GANG * 8, LANES)),
        in_specs=[smem] + [vmem] * 4,
        out_specs=vmem,
        scratch_shapes=[
            dense,
            pltpu.VMEM((BLOCKS, tall * HALF, LANES), F32),
            pltpu.VMEM((BLOCKS, tall, LANES), jnp.int32),
        ],
        compiler_params=params,
        cost_estimate=pl.CostEstimate(flops=8 * 10**9, bytes_accessed=16 * 10**6, transcendentals=0),
        name="backward",
    )(starts, packet, own, cas_back, returned)
    applied = lax.all_to_all(applied, BAND + ("l2",), 0, 0, tiled=True)
    each = pieces.shape[2] // LANES
    applied = applied.reshape(-1, 8, LANES)[:, :each].reshape(2 * trial.shape[0], -1)
    return applied, pieces[:, :-bands], jnp.concatenate([trial, theirs], axis=0)


def per_device(trial_block, all_bands, potential, positions, sphere_slots):
    applied, pieces, trial = apply_hamiltonian(
        trial_block, potential, positions, sphere_slots, all_bands
    )
    pieces = pieces.reshape(-1, pieces.shape[2])
    products = [
        jnp.einsum("ag,bg->ab", pieces, block, precision=lax.Precision.HIGH)
        for block in (trial, applied)
    ]
    products = jnp.concatenate(products, axis=1)
    columns = products.shape[1]
    near = lax.all_to_all(products, NEAR, 0, 0, tiled=True)
    near = jnp.sum(near.reshape(lax.axis_size(NEAR), -1, columns), axis=0)
    far = lax.all_to_all(near, ("l2", "ll"), 0, 0, tiled=True)
    total = jnp.sum(far, axis=0).reshape(2, -1)
    first = total[0].reshape(SIZES[1], SIZES[0], SIZES[2], -1)
    first = jnp.where(lax.axis_index("zh") == 0, first, first[::-1]).transpose(1, 0, 2, 3)
    return (first.reshape(1, -1), total[1:])


def solution(mesh):
    axes = Mesh(mesh.devices.reshape(SIZES), AXES)
    placed = (P(BAND, FFT), P(BAND, FFT), P(FFT, None, None), P(), P(FFT))
    return jax.shard_map(
        per_device,
        mesh=axes,
        in_specs=placed,
        out_specs=(P(BAND + FFT, None), P(BAND + FFT, None)),
        check_vma=False,
    )
```

```python
import functools
import math

import jax
import jax.numpy as jnp
import numpy as np
from jax import lax
from jax.experimental import pallas as pl
from jax.experimental.pallas import tpu as pltpu
from jax.sharding import Mesh
from jax.sharding import PartitionSpec as P

K = 64
LANES = 128
SIZES = (4, 2, 2, 4, 2, 4)
AXES = ("y", "zh", "c", "x", "l2", "ll")
BAND = ("y", "zh", "c")
FFT = ("x", "l2", "ll")
SIDE = ("y", "c")
NEAR = ("y", "c", "x")
GROUP = ("c", "x", "ll")
BLOCKS = 2
HALF = 4
GANG = BLOCKS * HALF
REACH_ROW, START_ROW, SLOT_ROW, ROWS = 196, 200, 204, 256
F32 = jnp.float32
BF16 = jnp.bfloat16


def cas_matrix(length):
    ids = np.arange(length)
    angle = (ids[:, None] * ids[None, :] % length) * (2.0 * math.pi / length)
    return ((np.cos(angle) + np.sin(angle)) / math.sqrt(length)).astype(np.float32)


def halves(table):
    high = table.astype(jnp.bfloat16)
    low = (table - high.astype(np.float32)).astype(jnp.bfloat16)
    return high, low


def split(values):
    high = values.astype(BF16)
    low = (values - high.astype(F32)).astype(BF16)
    return high, low


def dot(left, right):
    return jnp.dot(left, right, preferred_element_type=F32)


def wrapped(values, length):
    return jnp.where(values >= length // 2, values - length, values)


def take_lanes(row, lanes):
    return jnp.take_along_axis(row, lanes, axis=1, mode="promise_in_bounds")


def column_box(positions, grid_cells):
    first = lax.shift_right_logical(lax.shift_right_logical(positions, 6) * 43691, 17)
    second = positions - first * grid_cells
    return wrapped(first, grid_cells), wrapped(second, grid_cells)


def upper(size):
    ids = [lax.broadcasted_iota(jnp.int32, (size, size), axis) for axis in range(2)]
    return (ids[0] < ids[1]).astype(BF16)


def nt_dot(left, right):
    return lax.dot_general(left, right, (((1,), (1,)), ((), ())), preferred_element_type=F32)


def pack_kernel(
    grid_cells, half, slots_ref, trial_ref, own_ref, send_ref
):
    rows = slots_ref.shape[0]
    first_half = half[0] == 0
    column = slots_ref[...] & (LANES - 1)
    lane_ids = lax.broadcasted_iota(jnp.int32, (LANES, LANES), 0)
    ones = jnp.ones((8, LANES), BF16)
    total = jnp.zeros((8, LANES), F32)
    for row in range(rows):
        hit = (column[row : row + 1, :] == lane_ids).astype(BF16)
        total = total + nt_dot(ones, hit)
    reach = (total - 1.0) * 0.5
    padded = 2 * LANES
    height = lax.broadcasted_iota(jnp.int32, (padded, LANES), 0)
    away = jnp.abs(wrapped(height, grid_cells)).astype(F32)
    valid = ((away <= reach[0:1, :]) & (height < grid_cells)).astype(BF16)
    start = dot(nt_dot(ones, valid).astype(BF16), upper(padded))
    for row in range(rows):
        values = trial_ref[:, row * LANES : (row + 1) * LANES]
        own_ref[row * HALF : (row + 1) * HALF, :] = jnp.where(
            first_half, values[:HALF], values[HALF:]
        )
        send_ref[row * HALF : (row + 1) * HALF, :] = jnp.where(
            first_half, values[HALF:], values[:HALF]
        )
    own_slots = slots_ref[...].astype(F32)
    for packet_ref in (own_ref, send_ref):
        packet_ref[REACH_ROW : REACH_ROW + HALF, :] = reach[:HALF]
        packet_ref[START_ROW : START_ROW + 1, :] = start[:1, :LANES]
        packet_ref[START_ROW + 1 : START_ROW + 2, :] = start[:1, LANES:]
        packet_ref[START_ROW + 2 : SLOT_ROW, :] = jnp.zeros((2, LANES), F32)
        packet_ref[SLOT_ROW : SLOT_ROW + rows, :] = own_slots
        packet_ref[SLOT_ROW + rows :, :] = jnp.zeros((ROWS - SLOT_ROW - rows, LANES), F32)


def boxes_kernel(grid_cells, positions_ref, inverse_ref, box_ref):
    lane_ids = lax.broadcasted_iota(jnp.int32, (LANES, LANES), 0)
    first, second = column_box(positions_ref[...], grid_cells)
    box = (first + K // 2) * K + second + K // 2
    box_ref[...] = box
    sources = positions_ref.shape[0]
    blocks = sources
    block_ids = lax.broadcasted_iota(jnp.int32, (blocks, LANES), 0)
    own_lane = lax.broadcasted_iota(jnp.int32, (blocks, LANES), 1).astype(F32)
    inverse = jnp.zeros((2 * blocks, LANES), F32)
    for source in range(sources):
        place = box[source : source + 1, :]
        in_block = lax.shift_right_logical(place, 7) == block_ids
        left = jnp.concatenate(
            [jnp.where(in_block, float(source), 0.0), jnp.where(in_block, own_lane, 0.0)], axis=0
        ).astype(BF16)
        right = ((place & (LANES - 1)) == lane_ids).astype(BF16)
        inverse = inverse + nt_dot(left, right)
    inverse_ref[...] = inverse.astype(jnp.int32)


def z_transform(cas_ref, source_ref, out_ref, grid_cells):
    for block in range(0, GANG, 2):
        pair = jnp.concatenate(
            [source_ref[pl.ds(block + side, grid_cells, stride=GANG), :] for side in range(2)],
            axis=1,
        )
        high, low = split(pair)
        mixed = dot(cas_ref[...], jnp.concatenate([high, low, high], axis=0))
        for side in range(2):
            out_ref[pl.ds(block + side, grid_cells, stride=GANG), :] = mixed[
                :, side * LANES : (side + 1) * LANES
            ]


def forward_kernel(grid_cells, starts, packet_ref, cas_ref, out_ref, places, dense):
    height = lax.broadcasted_iota(jnp.int32, (grid_cells, LANES), 0)
    away = jnp.abs(wrapped(height, grid_cells)).astype(F32)
    ids = [lax.broadcasted_iota(jnp.int32, (grid_cells, grid_cells), axis) for axis in range(2)]
    below = (ids[0] > ids[1]).astype(BF16)
    before = upper(LANES)
    every = jnp.ones((LANES, LANES), BF16)
    for block in range(BLOCKS):
        row = block * ROWS + REACH_ROW
        valid = away <= packet_ref[row : row + 1, :]
        valid_one = valid.astype(BF16)
        rank = dot(valid_one, before).astype(jnp.int32)
        start = dot(below, dot(valid_one, every).astype(BF16)).astype(jnp.int32)
        place = jnp.where(valid, rank + (start & (LANES - 1)), -1)
        for band in range(HALF):
            places[pl.ds(block * HALF + band, grid_cells, stride=GANG), :] = place

    def expand(height, carry):
        rows = [
            block * ROWS + lax.shift_right_logical(starts[block, height], 7) * HALF
            for block in range(BLOCKS)
        ]
        rows = [pl.multiple_of(row, HALF) for row in rows]
        here = jnp.concatenate([packet_ref[pl.ds(row, HALF), :] for row in rows], axis=0)
        there = jnp.concatenate([packet_ref[pl.ds(row + HALF, HALF), :] for row in rows], axis=0)
        cut = pl.ds(pl.multiple_of(height * GANG, GANG), GANG)
        place = places[cut, :]
        lanes = place & (LANES - 1)
        value = jnp.where(place < LANES, take_lanes(here, lanes), take_lanes(there, lanes))
        dense[cut, :] = jnp.where(place < 0, 0.0, value)
        return carry

    lax.fori_loop(0, grid_cells, expand, 0, unroll=8)
    z_transform(cas_ref, dense, out_ref, grid_cells)


def potential_kernel(filter_ref, filter_t_ref, potential_ref, out_ref):
    for plane in range(potential_ref.shape[0]):
        high, low = split(potential_ref[plane])
        rows = dot(filter_ref[...], jnp.concatenate([high, low, high], axis=0))
        high, low = split(rows)
        out_ref[plane] = (
            dot(high, filter_t_ref[0]) + dot(low, filter_t_ref[0]) + dot(high, filter_t_ref[1])
        )


def plane_kernel(
    inverse_ref,
    box_ref,
    y_ref,
    x_ref,
    x_back_ref,
    y_back_ref,
    potential_ref,
    columns_ref,
    out_ref,
    boxes,
    staged,
    products,
):
    sources, planes, bands = staged.shape[:3]
    blocks = sources
    cores, runs = bands // HALF, SIZES[5]
    places = [
        (source, plane, core, (((core * SIZES[3] + x) * runs + run) * planes + plane) * GANG + block * HALF)
        for source, (x, block, run) in enumerate(np.ndindex(SIZES[3], BLOCKS, runs))
        for plane in range(planes)
        for core in range(cores)
    ]
    for source, plane, core, row in places:
        staged[source, plane, core * HALF : (core + 1) * HALF] = columns_ref[row : row + HALF, :]

    steps = products.shape[0]
    first_product = blocks - 2 * steps
    lane_rows = lax.broadcasted_iota(jnp.int32, (2 * LANES, 2 * LANES), 0)

    def stage_products(piece):
        for step in range(steps):
            for plane in range(0, planes, 2):
                sides = [
                    jnp.concatenate([piece(plane, at), piece(plane + 1, at)], axis=0)
                    for at in (first_product + 2 * step, first_product + 2 * step + 1)
                ]
                high, low = split(jnp.concatenate(sides, axis=1))
                products[step, plane * bands : (plane + 2) * bands, :] = high
                products[step, (planes + plane) * bands : (planes + plane + 2) * bands, :] = low

    def one_hot_part(wide):
        rest = jnp.zeros((2 * planes * bands, 2 * LANES), F32)
        for step in range(steps):
            low = (first_product + 2 * step) * LANES
            rest = rest + dot(products[step], (wide - low == lane_rows).astype(F32).astype(BF16))
        return rest[: planes * bands] + rest[planes * bands :]

    def gather_part(piece, from_of, lane_of):
        values = [jnp.zeros((bands, LANES), F32) for _ in range(planes)]
        for at in range(first_product):
            here = from_of == at
            for plane in range(planes):
                values[plane] = jnp.where(here, take_lanes(piece(plane, at), lane_of), values[plane])
        return values

    def column_piece(plane, source):
        return staged[source, plane]

    def box_piece(plane, block):
        return boxes[plane, block * bands : (block + 1) * bands, :]

    stage_products(column_piece)

    def fill(pair, carry):
        from_rows = [inverse_ref[pl.ds(pair * 2 + side, 1), :] for side in range(2)]
        lane_rows_of = [inverse_ref[pl.ds(pair * 2 + side + blocks, 1), :] for side in range(2)]
        wide = [from_rows[side] * LANES + lane_rows_of[side] for side in range(2)]
        rest = one_hot_part(jnp.concatenate(wide, axis=1))
        for side in range(2):
            from_of = jnp.broadcast_to(from_rows[side], (bands, LANES))
            lane_of = jnp.broadcast_to(lane_rows_of[side], (bands, LANES))
            values = gather_part(column_piece, from_of, lane_of)
            goal = pl.ds(pl.multiple_of((pair * 2 + side) * bands, bands), bands)
            for plane in range(planes):
                cut = slice(plane * bands, (plane + 1) * bands)
                boxes[plane, goal, :] = (
                    values[plane] + rest[cut, side * LANES : (side + 1) * LANES]
                )
        return carry

    lax.fori_loop(0, blocks // 2, fill, 0)

    def transform(plane, carry):
        stacked = jnp.concatenate(
            [boxes[plane, pl.ds(band, blocks, stride=bands), :] for band in range(bands)], axis=0
        )
        high, low = split(stacked)
        wide = dot(jnp.concatenate([high, low, high], axis=1), y_ref[...])
        potential = potential_ref[plane]
        potential = jnp.concatenate([potential, potential], axis=1)
        back = []
        for band in range(0, bands, 2):
            pair = []
            for one in (band, band + 1):
                mine = wide[one * blocks : (one + 1) * blocks, :]
                pair.append(jnp.concatenate([mine[:, :LANES], mine[:, LANES:]], axis=0))
            high, low = split(jnp.concatenate(pair, axis=1))
            field = dot(x_ref[...], jnp.concatenate([high, low, high], axis=0))
            high, low = split(field * potential)
            both = dot(x_back_ref[...], high)
            both = both[:K] + both[K:] + dot(x_back_ref[:K, :], low)
            for side in range(2):
                one = both[:, side * LANES : (side + 1) * LANES]
                back.append(jnp.concatenate([one[:blocks], one[blocks:]], axis=1))
        high, low = split(jnp.concatenate(back, axis=0))
        total = dot(high, y_back_ref[0]) + dot(low, y_back_ref[0]) + dot(high, y_back_ref[1])
        for band in range(bands):
            boxes[plane, pl.ds(band, blocks, stride=bands), :] = total[
                band * blocks : (band + 1) * blocks, :
            ]
        return carry

    lax.fori_loop(0, planes, transform, 0)

    stage_products(box_piece)

    def pick(pair, carry):
        places = [box_ref[pl.ds(pair * 2 + side, 1), :] for side in range(2)]
        rest = one_hot_part(jnp.concatenate(places, axis=1))
        for side in range(2):
            place = jnp.broadcast_to(places[side], (bands, LANES))
            values = gather_part(
                box_piece, lax.shift_right_logical(place, 7), place & (LANES - 1)
            )
            for plane in range(planes):
                cut = slice(plane * bands, (plane + 1) * bands)
                staged[pair * 2 + side, plane] = (
                    values[plane] + rest[cut, side * LANES : (side + 1) * LANES]
                )
        return carry

    lax.fori_loop(0, sources // 2, pick, 0)
    for source, plane, core, row in places:
        out_ref[row : row + HALF, :] = staged[source, plane, core * HALF : (core + 1) * HALF]


def backward_kernel(
    grid_cells, rows, starts, packet_ref, own_ref, cas_ref, returned_ref, out_ref, dense, packed, slots
):
    z_transform(cas_ref, returned_ref, dense, grid_cells)
    slots[...] = jnp.full(slots.shape, -1, jnp.int32)
    for block in range(BLOCKS):
        first = block * ROWS + SLOT_ROW
        slots[block, :rows] = packet_ref[first : first + rows, :].astype(jnp.int32)
    packed[...] = jnp.zeros_like(packed)

    def for_bands(rows_of):
        return jnp.concatenate([jnp.broadcast_to(row, (HALF, LANES)) for row in rows_of], axis=0)

    def compact(height, carry):
        values = dense[pl.ds(pl.multiple_of(height * GANG, GANG), GANG), :]
        for step in range(2):
            near = [
                lax.shift_right_logical(starts[block, height], 7) + step for block in range(BLOCKS)
            ]
            cuts = [pl.ds(pl.multiple_of(row * HALF, HALF), HALF) for row in near]
            own = for_bands([slots[block, pl.ds(near[block], 1), :] for block in range(BLOCKS)])
            old = jnp.concatenate([packed[block, cuts[block], :] for block in range(BLOCKS)], axis=0)
            mask = lax.shift_right_logical(own, 7) == height
            new = jnp.where(mask, take_lanes(values, own & (LANES - 1)), old)
            for block in range(BLOCKS):
                packed[block, cuts[block], :] = new[block * HALF : (block + 1) * HALF, :]
        return carry

    lax.fori_loop(0, grid_cells, compact, 0, unroll=8)
    first, second = column_box(own_ref[...], grid_cells)
    radial = (first * first + second * second).astype(F32)
    radial = for_bands([radial[block : block + 1, :] for block in range(BLOCKS)])
    parts = out_ref.shape[0] // (SIZES[1] * GANG * 8)
    each = -(-rows // parts)
    for part in range(parts):
        for place in range(8):
            row = part * each + place
            if place >= each or row >= rows:
                value = jnp.zeros((GANG, LANES), F32)
            else:
                own = for_bands([slots[block, row : row + 1, :] for block in range(BLOCKS)])
                height = wrapped(lax.shift_right_logical(own, 7), grid_cells)
                around = take_lanes(radial, own & (LANES - 1))
                kinetic = 2.0 * (around + (height * height).astype(F32)) / (K * K)
                cut = slice(row * HALF, (row + 1) * HALF)
                trial = jnp.concatenate(
                    [packet_ref[block * ROWS + cut.start : block * ROWS + cut.stop, :] for block in range(BLOCKS)],
                    axis=0,
                )
                value = jnp.concatenate([packed[block, cut, :] for block in range(BLOCKS)], axis=0)
                value = value + kinetic * trial
            for zh in range(SIZES[1]):
                to = (part // SIZES[2] * SIZES[1] + zh) * SIZES[2] + part % SIZES[2]
                out_ref[pl.ds(to * GANG * 8 + place, GANG, stride=8), :] = value


def constant_tables(grid_cells):
    fine = 2 * K
    order = np.arange(grid_cells).reshape(SIZES[3], SIZES[2], SIZES[5], -1)
    order = order.transpose(1, 0, 2, 3).reshape(-1)
    high, low = halves(cas_matrix(grid_cells))
    cas_out = np.concatenate([high[order], high[order], low[order]], axis=1)
    cas_back = np.concatenate([high[:, order], high[:, order], low[:, order]], axis=1)
    theta = (np.arange(fine) + 0.5) / fine
    full = np.arange(grid_cells) / grid_cells
    box = np.arange(K) - K // 2
    angle = 2.0 * math.pi * box[:, None] * theta[None, :]
    box_table = ((np.cos(angle) + np.sin(angle)) / math.sqrt(fine)).astype(np.float32)
    waves = 2.0 * math.pi * np.arange(1, K)
    apart = theta[:, None] - full[None, :]
    project = 1.0 + 2.0 * np.cos(waves[:, None, None] * apart[None]).sum(axis=0)
    edge = 2.0 * math.pi * K
    project = project + np.sin(edge * theta)[:, None] * np.sin(edge * full)[None, :]
    project = (project / grid_cells).astype(np.float32)
    high, low = halves(project)
    filter_three = np.concatenate([high, high, low], axis=1)
    filter_back = np.stack([high.T, low.T])
    sides = np.zeros((2, K, 2, fine), np.float32)
    for side in range(2):
        sides[side, :, side, :] = box_table
    high, low = halves(sides.reshape(2 * K, 2 * fine))
    y_three = np.concatenate([high, high, low], axis=0)
    y_back = np.stack([high.T, low.T])
    order = np.concatenate([np.arange(0, K, 2), np.arange(1, K, 2)])
    high, low = halves(box_table[order])
    x_three = np.concatenate([high, high, low], axis=0).T
    x_back = np.concatenate([high, low], axis=0)
    tables = (cas_out, cas_back, filter_three, filter_back, y_three, x_three, x_back, y_back)
    return tuple(jnp.asarray(one) for one in tables)


def swap_pairs(turn):
    place = np.arange(math.prod(SIZES)).reshape(SIZES)
    pairs = []
    for (y, zh, c, x, l2, ll), target in np.ndenumerate(place):
        near = zh if l2 == c else (zh * 2 + l2 + turn) % 4 // 2
        pairs.append((int(place[y, near, l2, x, c, ll]), int(target)))
    return tuple(pairs)


def swapped(block, axis):
    return lax.ppermute(block, axis, ((0, 1), (1, 0)))


def arrange(block):
    parts = lax.axis_size(SIDE)
    width = -(-block.shape[1] // (LANES * parts)) * LANES
    block = jnp.pad(block, ((0, 0), (0, parts * width - block.shape[1])))
    return block.reshape(-1, parts, width).transpose(1, 0, 2)


def apply_hamiltonian(trial_block, potential, positions, sphere_slots, all_bands):
    bands, coefs = trial_block.shape
    planes, grid_cells = potential.shape[:2]
    fft_size = lax.axis_size(FFT)
    rows = coefs // LANES
    slots = sphere_slots.reshape(rows, LANES)
    position_rows = positions.reshape(fft_size, LANES)
    own = position_rows.reshape(SIZES[3], BLOCKS, SIZES[5], LANES)
    own = lax.dynamic_index_in_dim(own, lax.axis_index("x"), 0, keepdims=False)
    own = lax.dynamic_index_in_dim(own, lax.axis_index("ll"), 1, keepdims=False)
    cas_out, cas_back, filter_three, filter_back, *plane_tables = constant_tables(grid_cells)
    i32 = functools.partial(jax.ShapeDtypeStruct, dtype=jnp.int32)
    f32 = functools.partial(jax.ShapeDtypeStruct, dtype=F32)
    params = pltpu.CompilerParams(vmem_limit_bytes=48 * 2**20)
    smem = pl.BlockSpec(memory_space=pltpu.SMEM)
    vmem = pl.BlockSpec(memory_space=pltpu.VMEM)
    half = lax.axis_index("l2")
    packet = f32((ROWS, LANES))
    kept, sent = pl.pallas_call(
        functools.partial(pack_kernel, grid_cells),
        out_shape=(packet, packet),
        in_specs=[smem] + [vmem] * 2,
        out_specs=[vmem] * 2,
        compiler_params=params,
        name="pack",
    )(half.reshape(1), slots, trial_block)
    sent, potential, pieces, position_rows = lax.optimization_barrier(
        (sent, potential, all_bands, position_rows)
    )
    other = swapped(sent, "l2")
    pieces = arrange(jnp.concatenate([pieces, trial_block], axis=0))
    inverse, box = pl.pallas_call(
        functools.partial(boxes_kernel, grid_cells),
        out_shape=(i32((2 * fft_size, LANES)), i32((fft_size, LANES))),
        compiler_params=params,
        name="boxes",
    )(position_rows)
    filtered = pl.pallas_call(
        potential_kernel,
        out_shape=f32((planes, 2 * K, 2 * K)),
        compiler_params=params,
        name="filter",
    )(filter_three, filter_back, potential)
    cut = planes // 2
    filtered = [
        lax.ppermute(part, BAND + FFT, swap_pairs(turn))
        for part, turn in ((filtered[:cut], 1), (filtered[cut:], -1))
    ]
    packet = jnp.where(half == 0, jnp.stack([kept, other]), jnp.stack([other, kept]))
    starts = packet[:, START_ROW : START_ROW + 2].reshape(BLOCKS, -1).astype(jnp.int32)
    packet = packet.reshape(BLOCKS * ROWS, LANES)
    dense_rows = grid_cells * GANG
    dense = pltpu.VMEM((dense_rows, LANES), F32)
    mixed = pl.pallas_call(
        functools.partial(forward_kernel, grid_cells),
        out_shape=f32((dense_rows, LANES)),
        in_specs=[smem, vmem, vmem],
        out_specs=vmem,
        scratch_shapes=[pltpu.VMEM((dense_rows, LANES), jnp.int32), dense],
        compiler_params=params,
        name="forward",
    )(starts, packet, cas_out)
    filtered = jnp.concatenate(filtered, axis=0)
    pieces = lax.all_to_all(pieces, SIDE, 0, 0, tiled=True)
    mixed, filtered, pieces = lax.optimization_barrier((mixed, filtered, pieces))
    gathered = lax.all_to_all(mixed, GROUP, 0, 0, tiled=True)
    trial = pieces[:, -bands:].reshape(-1, pieces.shape[2])
    theirs = swapped(trial, "zh")
    weighted = pl.pallas_call(
        plane_kernel,
        out_shape=f32(gathered.shape),
        scratch_shapes=[
            pltpu.VMEM((planes, fft_size * bands, LANES), F32),
            pltpu.VMEM((fft_size, planes, bands, LANES), F32),
            pltpu.VMEM((8, 2 * planes * bands, 2 * LANES), BF16),
        ],
        compiler_params=params,
        cost_estimate=pl.CostEstimate(
            flops=25 * 10**9, bytes_accessed=60 * 10**6, transcendentals=0
        ),
        name="planes",
    )(inverse, box, *plane_tables, filtered, gathered)
    weighted, theirs = lax.optimization_barrier((weighted, theirs))
    returned = lax.all_to_all(weighted, GROUP, 0, 0, tiled=True)
    parts = pieces.shape[0]
    tall = rows + 7 & -8
    applied = pl.pallas_call(
        functools.partial(backward_kernel, grid_cells, rows),
        out_shape=f32((SIZES[1] * parts * GANG * 8, LANES)),
        in_specs=[smem] + [vmem] * 4,
        out_specs=vmem,
        scratch_shapes=[
            dense,
            pltpu.VMEM((BLOCKS, tall * HALF, LANES), F32),
            pltpu.VMEM((BLOCKS, tall, LANES), jnp.int32),
        ],
        compiler_params=params,
        cost_estimate=pl.CostEstimate(flops=8 * 10**9, bytes_accessed=16 * 10**6, transcendentals=0),
        name="backward",
    )(starts, packet, own, cas_back, returned)
    applied = lax.all_to_all(applied, BAND + ("l2",), 0, 0, tiled=True)
    each = pieces.shape[2] // LANES
    applied = applied.reshape(-1, 8, LANES)[:, :each].reshape(2 * trial.shape[0], -1)
    return applied, pieces[:, :-bands], jnp.concatenate([trial, theirs], axis=0)


def per_device(trial_block, all_bands, potential, positions, sphere_slots):
    applied, pieces, trial = apply_hamiltonian(
        trial_block, potential, positions, sphere_slots, all_bands
    )
    pieces = pieces.reshape(-1, pieces.shape[2])
    products = [
        jnp.einsum("ag,bg->ab", pieces, block, precision=lax.Precision.HIGH)
        for block in (trial, applied)
    ]
    products = jnp.concatenate(products, axis=1)
    columns = products.shape[1]
    near = lax.all_to_all(products, NEAR, 0, 0, tiled=True)
    near = jnp.sum(near.reshape(lax.axis_size(NEAR), -1, columns), axis=0)
    far = lax.all_to_all(near, ("l2", "ll"), 0, 0, tiled=True)
    total = jnp.sum(far, axis=0).reshape(2, -1)
    first = total[0].reshape(SIZES[1], SIZES[0], SIZES[2], -1)
    first = jnp.where(lax.axis_index("zh") == 0, first, first[::-1]).transpose(1, 0, 2, 3)
    return (first.reshape(1, -1), total[1:])


def solution(mesh):
    axes = Mesh(mesh.devices.reshape(SIZES), AXES)
    placed = (P(BAND, FFT), P(BAND, FFT), P(FFT, None, None), P(), P(FFT))
    return jax.shard_map(
        per_device,
        mesh=axes,
        in_specs=placed,
        out_specs=(P(BAND + FFT, None), P(BAND + FFT, None)),
        check_vma=False,
    )
```
